512 devices in a mesh: pair: 32 (over z_lo, y), virt: 16 (over z_hi, x, core).
Axes of the slice: x: 4, y: 4, z: 16 (z_hi: 2, z_lo: 8; z = z_hi * 8 + z_lo), core: 2. Of those that a mesh axis runs over, the one named last changes fastest.
Arguments:
- lambda_amps: bfloat16 [384, 1024, 1024], P('pair', 'virt'), may hold values from -0.0002975464 to 0.0002975464
- t_amps: bfloat16 [384, 1024, 1024], P('pair', 'virt'), may hold values from -6 to 6
- panel_home: int32 [32], replicated, may hold values from 0 to 31, each once
- pair_list: int32 [264, 2], replicated, may hold values from 0 to 31, as said below
Outputs:
- density: bfloat16 [384, 1024, 1024], P('pair', 'virt')
The draws below stay inside these ranges and needn't reach their ends.
Inputs may be any that keep to these rules, and one draw needn't show every extreme that they name: `pair_list`: rows are distinct panel pairs with first entry <= second.
All inputs are finite; a program needn't handle non-finite values.
Results may differ from the reference program's by a relative error of at most 0.0049.
Values may be sent and summed in bfloat16 or wider, within the bound.
No kernel may reach another device: no remote copies, remote signals or barrier semaphores. Data moves between devices by JAX's collectives and lax.ppermute only.
A program may use at most 64 MiB of HBM per device.

```python
import jax
import jax.numpy as jnp
import numpy as np
from jax import lax

V = 1024
PAN = 12
NPAN = 32
PAIRS = 384
NLIST = 264


def draw_pair_list(key, part):
    key = jax.random.fold_in(key, 7)
    rows, cols = np.triu_indices(NPAN)
    order = jax.random.permutation(key, rows.shape[0])[:NLIST]
    first = jnp.asarray(rows, jnp.int32)[order]
    second = jnp.asarray(cols, jnp.int32)[order]
    return jnp.stack([first, second], axis=1)


def steps_of(stream_key, shape, cuts, low, top_value):
    def one(axis_at, blocks):
        steps = jax.random.uniform(jax.random.fold_in(jax.random.fold_in(stream_key, 6), axis_at), (blocks,), jnp.float32, low / len(cuts), top_value / len(cuts))
        return jnp.repeat(jnp.exp(steps), shape[axis_at] // blocks).reshape((-1,) + (1,) * (len(shape) - axis_at - 1))

    level = one(*cuts[0])
    for cut in cuts[1:]:
        level = level * one(*cut)
    return level


def bell_draw(key, dims, spread, limit, pieces=(), held_as=jnp.bfloat16):
    drawn = jax.random.normal(key, dims, jnp.float32) * spread
    if len(pieces) > 0:
        drawn = steps_of(key, dims, pieces, -0.22, 0.18) * drawn
    return jnp.clip(drawn, min=-limit, max=limit).astype(held_as)


def setup_inputs(seed: int = 0) -> dict:
    streams_of = jax.random.split(jax.random.key(seed), 5)
    return {
        "lambda_amps": bell_draw(streams_of[0], (PAIRS, V, V), (1.0 / (V * PAIRS ** 0.5)), 0.0002975464, ((0, 32), (1, 16))),
        "t_amps": bell_draw(streams_of[1], (PAIRS, V, V), 1.0, 6.0, ((0, 32), (1, 16))),
        "panel_home": jax.random.permutation(streams_of[2], NPAN).astype(jnp.int32),
        "pair_list": draw_pair_list(jax.random.fold_in(streams_of[4], 71), 0),
    }


def onehot(index, count):
    return (index[:, None] == jnp.arange(count)[None, :]).astype(jnp.float32)


def build_mask(panel_home, pair_list):
    home = onehot(panel_home, NPAN)
    first = jnp.dot(onehot(pair_list[:, 0], NPAN), home, precision=lax.Precision.HIGHEST)
    second = jnp.dot(onehot(pair_list[:, 1], NPAN), home, precision=lax.Precision.HIGHEST)
    panels = jnp.dot(first.T, second, precision=lax.Precision.HIGHEST)
    panels = jnp.minimum(panels + panels.T, 1.0)
    return jnp.repeat(jnp.repeat(panels, PAN, axis=0), PAN, axis=1)


def reference(lambda_amps, t_amps, panel_home, pair_list):
    lam = lambda_amps.reshape(PAIRS, V * V)
    amp = t_amps.reshape(PAIRS, V * V)
    cross = lax.dot_general(lam, amp, (((1,), (1,)), ((), ())), preferred_element_type=jnp.float32)
    inter = (build_mask(panel_home, pair_list) * 0.5 * (cross + cross.T)).astype(jnp.bfloat16)
    blocks = amp.reshape(PAIRS, 16, (V * V) // 16).transpose(1, 0, 2)

    def apply_block(piece):
        return jnp.dot(inter, piece, preferred_element_type=jnp.float32).astype(jnp.bfloat16)

    out = lax.map(apply_block, blocks)
    return out.transpose(1, 0, 2).reshape(PAIRS, V, V)
```

```python
import jax
import jax.numpy as jnp
from jax import lax
from jax.experimental import pallas as pl
from jax.experimental.pallas import tpu as pltpu
from jax.sharding import PartitionSpec as P

ROWS = 16
LANES = 128
BLOCK = 128
VMEM_LIMIT = 48 * 1024 * 1024


def onehot(index, count):
    return (index[:, None] == jnp.arange(count)[None, :]).astype(jnp.float32)


def vmem(count):
    return [pl.BlockSpec(memory_space=pltpu.VMEM)] * count


def call(body, out_shape, args, scratch=()):
    outs = out_shape if isinstance(out_shape, (list, tuple)) else [out_shape]
    specs = vmem(len(outs))
    return pl.pallas_call(
        body,
        out_shape=out_shape,
        in_specs=vmem(len(args)),
        out_specs=specs if isinstance(out_shape, (list, tuple)) else specs[0],
        scratch_shapes=list(scratch),
        compiler_params=pltpu.CompilerParams(vmem_limit_bytes=VMEM_LIMIT),
    )(*args)


def pack(lam_ref, amp_ref, out_ref):
    down, across = lam_ref.shape[1] // ROWS, lam_ref.shape[2] // LANES
    for i in range(down):
        for c in range(across):
            part = (slice(None), slice(i * ROWS, (i + 1) * ROWS), slice(c * LANES, (c + 1) * LANES))
            out_ref[i * across + c, 0] = lam_ref[part]
            out_ref[i * across + c, 1] = amp_ref[part]


def unpack(parts_ref, out_ref):
    down, across = out_ref.shape[1] // ROWS, out_ref.shape[2] // LANES
    for i in range(down):
        for c in range(across):
            out_ref[:, i * ROWS : (i + 1) * ROWS, c * LANES : (c + 1) * LANES] = parts_ref[i * across + c]


def swap_matrix():
    side = ROWS * ROWS
    i = lax.broadcasted_iota(jnp.int32, (side, side), 0)
    j = lax.broadcasted_iota(jnp.int32, (side, side), 1)
    return (j == (i % ROWS) * ROWS + i // ROWS).astype(jnp.float32).astype(jnp.bfloat16)


def upper_blocks(pairs):
    n = pairs // BLOCK
    return [(i, j) for i in range(n) for j in range(i, n)]


def cross_kernel(parts_ref, sym_ref, amp_ref, lam_ref):
    swap = swap_matrix()
    panels, _, panel_size = parts_ref.shape[:3]
    side = ROWS * ROWS
    chunk = 4 * panel_size

    def relayout(step, carry):
        lam = parts_ref[pl.ds(4 * step, 4), 0].reshape(chunk * ROWS, LANES)
        amp = parts_ref[pl.ds(4 * step, 4), 1].reshape(chunk * ROWS, LANES)
        both = jnp.concatenate([lam, amp], axis=1)
        for q in range(chunk // ROWS):
            moved = jnp.dot(swap, both[q * side : (q + 1) * side], preferred_element_type=jnp.float32)
            moved = moved.astype(jnp.bfloat16)
            at = pl.ds(pl.multiple_of(step * chunk + q * ROWS, ROWS), ROWS)
            for s in range(ROWS):
                lam_ref[at, s * LANES : (s + 1) * LANES] = moved[s * ROWS : (s + 1) * ROWS, :LANES]
                amp_ref[at, s * LANES : (s + 1) * LANES] = moved[s * ROWS : (s + 1) * ROWS, LANES:]
        return carry

    lax.fori_loop(0, panels // 4, relayout, 0)
    cross = lax.dot_general(
        lam_ref[...], amp_ref[...], (((1,), (1,)), ((), ())), preferred_element_type=jnp.float32
    )
    sym = 0.5 * (cross + cross.T)
    for n, (i, j) in enumerate(upper_blocks(cross.shape[0])):
        sym_ref[n * BLOCK : (n + 1) * BLOCK] = sym[i * BLOCK : (i + 1) * BLOCK, j * BLOCK : (j + 1) * BLOCK]


def density_kernel(upper_ref, listed_ref, amp_ref, out_ref, inter_ref, flat_ref):
    pairs, depth = amp_ref.shape
    panels = listed_ref.shape[0]
    panel_size = pairs // panels
    row = lax.broadcasted_iota(jnp.int32, (pairs, panels), 0)
    first = lax.broadcasted_iota(jnp.int32, (pairs, panels), 1) * panel_size
    spread = ((row >= first) & (row < first + panel_size)).astype(jnp.float32)
    mask = jnp.dot(spread, listed_ref[...], preferred_element_type=jnp.float32)
    mask = lax.dot_general(mask, spread, (((1,), (1,)), ((), ())), preferred_element_type=jnp.float32)
    for n, (i, j) in enumerate(upper_blocks(pairs)):
        block = upper_ref[n * BLOCK : (n + 1) * BLOCK].astype(jnp.float32)
        rows, cols = slice(i * BLOCK, (i + 1) * BLOCK), slice(j * BLOCK, (j + 1) * BLOCK)
        inter_ref[rows, cols] = (block * mask[rows, cols]).astype(jnp.bfloat16)
        if i != j:
            inter_ref[cols, rows] = (block.T * mask[cols, rows]).astype(jnp.bfloat16)
    wide = 2 * LANES
    for c in range(depth // wide):
        flat_ref[:, c * wide : (c + 1) * wide] = jnp.dot(
            inter_ref[...], amp_ref[:, c * wide : (c + 1) * wide], preferred_element_type=jnp.float32
        ).astype(jnp.bfloat16)
    swap = swap_matrix()

    def relayout(step, carry):
        at = pl.multiple_of(step * 2 * ROWS, 2 * ROWS)
        halves = []
        for h in range(2):
            rows = pl.ds(at + h * ROWS, ROWS)
            halves.append(
                jnp.concatenate([flat_ref[rows, s * LANES : (s + 1) * LANES] for s in range(ROWS)], axis=0)
            )
        moved = jnp.dot(swap, jnp.concatenate(halves, axis=1), preferred_element_type=jnp.float32)
        moved = moved.astype(jnp.bfloat16)
        for h in range(2):
            out_ref[pl.ds(at + h * ROWS, ROWS)] = moved[:, h * LANES : (h + 1) * LANES].reshape(ROWS, ROWS, LANES)
        return carry

    lax.fori_loop(0, pairs // (2 * ROWS), relayout, 0)


def exchange(x, axis):
    return lax.all_to_all(x, axis, split_axis=0, concat_axis=0, tiled=True)


def on_device(lambda_amps, t_amps, panel_home, pair_list):
    npanels = lax.axis_size("pair")
    nslabs = lax.axis_size("virt")
    panel_size, rows, cols = lambda_amps.shape
    pairs = npanels * panel_size
    depth = rows * cols // npanels
    bf16, f32 = jnp.bfloat16, jnp.float32

    home = onehot(panel_home, npanels)
    first = jnp.dot(onehot(pair_list[:, 0], npanels), home, precision=lax.Precision.HIGHEST)
    second = jnp.dot(onehot(pair_list[:, 1], npanels), home, precision=lax.Precision.HIGHEST)
    listed = jnp.dot(first.T, second, precision=lax.Precision.HIGHEST)
    listed = jnp.minimum(listed + listed.T, 1.0)

    parts = call(
        pack,
        jax.ShapeDtypeStruct((npanels, 2, panel_size, ROWS, LANES), bf16),
        (lambda_amps, t_amps),
    )
    parts = exchange(parts, "pair")
    nblocks = len(upper_blocks(pairs))
    sym, amp = call(
        cross_kernel,
        [
            jax.ShapeDtypeStruct((nblocks * BLOCK, BLOCK), f32),
            jax.ShapeDtypeStruct((pairs, depth), bf16),
        ],
        (parts,),
        [pltpu.VMEM((pairs, depth), bf16)],
    )
    own = nblocks * BLOCK // npanels
    terms = exchange(sym.reshape(npanels, own, BLOCK), "pair")
    terms = jnp.broadcast_to(jnp.sum(terms, axis=0), (nslabs, own, BLOCK))
    total = jnp.sum(exchange(terms, "virt"), axis=0).astype(bf16)
    upper = exchange(jnp.broadcast_to(total, (npanels, own, BLOCK)), "pair")
    result = call(
        density_kernel,
        jax.ShapeDtypeStruct((pairs, ROWS, LANES), bf16),
        (upper.reshape(nblocks * BLOCK, BLOCK), listed, amp),
        [pltpu.VMEM((pairs, pairs), bf16), pltpu.VMEM((pairs, depth), bf16)],
    )
    result = exchange(result.reshape(npanels, panel_size, ROWS, LANES), "pair")
    return call(unpack, jax.ShapeDtypeStruct(lambda_amps.shape, bf16), (result,))


def solution(mesh):
    placed = (P("pair", "virt", None), P("pair", "virt", None), P(), P())
    return jax.shard_map(
        on_device, mesh=mesh, in_specs=placed, out_specs=P("pair", "virt", None), check_vma=False
    )
```

```python
import jax
import jax.numpy as jnp
from jax import lax
from jax.experimental import pallas as pl
from jax.experimental.pallas import tpu as pltpu
from jax.sharding import Mesh, PartitionSpec as P

PAIR = ("zl", "y")
VIRT = ("zh", "x", "c")
PLANE = ("y", "x", "c")
LINE = ("zl", "zh")

ROWS = 16
LANES = 128
BLOCK = 128
VMEM_LIMIT = 48 * 1024 * 1024


def onehot(index, count):
    return (index[:, None] == jnp.arange(count)[None, :]).astype(jnp.float32)


def vmem(count):
    return [pl.BlockSpec(memory_space=pltpu.VMEM)] * count


def call(body, out_shape, args, scratch=()):
    outs = out_shape if isinstance(out_shape, (list, tuple)) else [out_shape]
    specs = vmem(len(outs))
    return pl.pallas_call(
        body,
        out_shape=out_shape,
        in_specs=vmem(len(args)),
        out_specs=specs if isinstance(out_shape, (list, tuple)) else specs[0],
        scratch_shapes=list(scratch),
        compiler_params=pltpu.CompilerParams(vmem_limit_bytes=VMEM_LIMIT),
    )(*args)


def pack(lam_ref, amp_ref, out_ref):
    down, across = lam_ref.shape[1] // ROWS, lam_ref.shape[2] // LANES
    for i in range(down):
        for c in range(across):
            part = (slice(None), slice(i * ROWS, (i + 1) * ROWS), slice(c * LANES, (c + 1) * LANES))
            out_ref[i * across + c, 0] = lam_ref[part]
            out_ref[i * across + c, 1] = amp_ref[part]


def unpack(parts_ref, out_ref):
    down, across = out_ref.shape[1] // ROWS, out_ref.shape[2] // LANES
    for i in range(down):
        for c in range(across):
            out_ref[:, i * ROWS : (i + 1) * ROWS, c * LANES : (c + 1) * LANES] = parts_ref[i * across + c]


def swap_matrix():
    side = ROWS * ROWS
    i = lax.broadcasted_iota(jnp.int32, (side, side), 0)
    j = lax.broadcasted_iota(jnp.int32, (side, side), 1)
    return (j == (i % ROWS) * ROWS + i // ROWS).astype(jnp.float32).astype(jnp.bfloat16)


def upper_blocks(pairs):
    n = pairs // BLOCK
    return [(i, j) for i in range(n) for j in range(i, n)]


def cross_kernel(parts_ref, sym_ref, amp_ref, lam_ref):
    swap = swap_matrix()
    panels, _, panel_size = parts_ref.shape[:3]
    side = ROWS * ROWS
    chunk = 4 * panel_size

    def relayout(step, carry):
        lam = parts_ref[pl.ds(4 * step, 4), 0].reshape(chunk * ROWS, LANES)
        amp = parts_ref[pl.ds(4 * step, 4), 1].reshape(chunk * ROWS, LANES)
        both = jnp.concatenate([lam, amp], axis=1)
        for q in range(chunk // ROWS):
            moved = jnp.dot(swap, both[q * side : (q + 1) * side], preferred_element_type=jnp.float32)
            moved = moved.astype(jnp.bfloat16)
            at = pl.ds(pl.multiple_of(step * chunk + q * ROWS, ROWS), ROWS)
            for s in range(ROWS):
                lam_ref[at, s * LANES : (s + 1) * LANES] = moved[s * ROWS : (s + 1) * ROWS, :LANES]
                amp_ref[at, s * LANES : (s + 1) * LANES] = moved[s * ROWS : (s + 1) * ROWS, LANES:]
        return carry

    lax.fori_loop(0, panels // 4, relayout, 0)
    cross = lax.dot_general(
        lam_ref[...], amp_ref[...], (((1,), (1,)), ((), ())), preferred_element_type=jnp.float32
    )
    sym = 0.5 * (cross + cross.T)
    for n, (i, j) in enumerate(upper_blocks(cross.shape[0])):
        sym_ref[n * BLOCK : (n + 1) * BLOCK] = sym[i * BLOCK : (i + 1) * BLOCK, j * BLOCK : (j + 1) * BLOCK]


def density_kernel(upper_ref, listed_ref, amp_ref, out_ref, inter_ref, flat_ref):
    pairs, depth = amp_ref.shape
    panels = listed_ref.shape[0]
    panel_size = pairs // panels
    row = lax.broadcasted_iota(jnp.int32, (pairs, panels), 0)
    first = lax.broadcasted_iota(jnp.int32, (pairs, panels), 1) * panel_size
    spread = ((row >= first) & (row < first + panel_size)).astype(jnp.float32)
    mask = jnp.dot(spread, listed_ref[...], preferred_element_type=jnp.float32)
    mask = lax.dot_general(mask, spread, (((1,), (1,)), ((), ())), preferred_element_type=jnp.float32)
    for n, (i, j) in enumerate(upper_blocks(pairs)):
        block = upper_ref[n * BLOCK : (n + 1) * BLOCK].astype(jnp.float32)
        rows, cols = slice(i * BLOCK, (i + 1) * BLOCK), slice(j * BLOCK, (j + 1) * BLOCK)
        inter_ref[rows, cols] = (block * mask[rows, cols]).astype(jnp.bfloat16)
        if i != j:
            inter_ref[cols, rows] = (block.T * mask[cols, rows]).astype(jnp.bfloat16)
    wide = 2 * LANES
    for c in range(depth // wide):
        flat_ref[:, c * wide : (c + 1) * wide] = jnp.dot(
            inter_ref[...], amp_ref[:, c * wide : (c + 1) * wide], preferred_element_type=jnp.float32
        ).astype(jnp.bfloat16)
    swap = swap_matrix()

    def relayout(step, carry):
        at = pl.multiple_of(step * 2 * ROWS, 2 * ROWS)
        halves = []
        for h in range(2):
            rows = pl.ds(at + h * ROWS, ROWS)
            halves.append(
                jnp.concatenate([flat_ref[rows, s * LANES : (s + 1) * LANES] for s in range(ROWS)], axis=0)
            )
        moved = jnp.dot(swap, jnp.concatenate(halves, axis=1), preferred_element_type=jnp.float32)
        moved = moved.astype(jnp.bfloat16)
        for h in range(2):
            out_ref[pl.ds(at + h * ROWS, ROWS)] = moved[:, h * LANES : (h + 1) * LANES].reshape(ROWS, ROWS, LANES)
        return carry

    lax.fori_loop(0, pairs // (2 * ROWS), relayout, 0)


def exchange(x, axis):
    return lax.all_to_all(x, axis, split_axis=0, concat_axis=0, tiled=True)


def on_device(lambda_amps, t_amps, panel_home, pair_list):
    npanels = lax.axis_size(PAIR)
    panel_size, rows, cols = lambda_amps.shape
    pairs = npanels * panel_size
    depth = rows * cols // npanels
    bf16, f32 = jnp.bfloat16, jnp.float32

    home = onehot(panel_home, npanels)
    first = jnp.dot(onehot(pair_list[:, 0], npanels), home, precision=lax.Precision.HIGHEST)
    second = jnp.dot(onehot(pair_list[:, 1], npanels), home, precision=lax.Precision.HIGHEST)
    listed = jnp.dot(first.T, second, precision=lax.Precision.HIGHEST)
    listed = jnp.minimum(listed + listed.T, 1.0)

    parts = call(
        pack,
        jax.ShapeDtypeStruct((npanels, 2, panel_size, ROWS, LANES), bf16),
        (lambda_amps, t_amps),
    )
    parts = exchange(parts, PAIR)
    nblocks = len(upper_blocks(pairs))
    sym, amp = call(
        cross_kernel,
        [
            jax.ShapeDtypeStruct((nblocks * BLOCK, BLOCK), f32),
            jax.ShapeDtypeStruct((pairs, depth), bf16),
        ],
        (parts,),
        [pltpu.VMEM((pairs, depth), bf16)],
    )
    plane, height = lax.axis_size(PLANE), lax.axis_size(LINE)
    own = nblocks * BLOCK // plane
    terms = exchange(sym.reshape(plane, own, BLOCK), PLANE)
    terms = jnp.broadcast_to(jnp.sum(terms, axis=0), (height, own, BLOCK))
    total = jnp.sum(exchange(terms, LINE), axis=0).astype(bf16)
    upper = exchange(jnp.broadcast_to(total, (plane, own, BLOCK)), PLANE)
    result = call(
        density_kernel,
        jax.ShapeDtypeStruct((pairs, ROWS, LANES), bf16),
        (upper.reshape(nblocks * BLOCK, BLOCK), listed, amp),
        [pltpu.VMEM((pairs, pairs), bf16), pltpu.VMEM((pairs, depth), bf16)],
    )
    result = exchange(result.reshape(npanels, panel_size, ROWS, LANES), PAIR)
    return call(unpack, jax.ShapeDtypeStruct(lambda_amps.shape, bf16), (result,))


def solution(mesh):
    fine = Mesh(mesh.devices.reshape(8, 4, 2, 4, 2), PAIR + VIRT)
    placed = (P(PAIR, VIRT, None), P(PAIR, VIRT, None), P(), P())
    return jax.shard_map(
        on_device, mesh=fine, in_specs=placed, out_specs=P(PAIR, VIRT, None), check_vma=False
    )
```

```python
import jax
import jax.numpy as jnp
from jax import lax
from jax.experimental import pallas as pl
from jax.experimental.pallas import tpu as pltpu
from jax.sharding import Mesh, PartitionSpec as P

HALF = ("z4", "y")
PAIR = ("zb",) + HALF
VIRT = ("zh", "x", "c")
PLANE = ("y", "x", "c")
LINE = ("zb", "z4", "zh")

ROWS = 16
LANES = 128
TILES = 2
WIDE = TILES * LANES
SIDE = ROWS * ROWS
STEPS = 4
BLOCK = 128
VMEM_LIMIT = 48 * 1024 * 1024


def onehot(index, count):
    return (index[:, None] == jnp.arange(count)[None, :]).astype(jnp.float32)


def call(body, out_shape, args, scratch=(), scalars=0):
    many = isinstance(out_shape, (list, tuple))
    outs = out_shape if many else [out_shape]
    smem, vmem = (pl.BlockSpec(memory_space=m) for m in (pltpu.SMEM, pltpu.VMEM))
    return pl.pallas_call(
        body,
        out_shape=out_shape,
        in_specs=[smem] * scalars + [vmem] * (len(args) - scalars),
        out_specs=[vmem] * len(outs) if many else vmem,
        scratch_shapes=list(scratch),
        compiler_params=pltpu.CompilerParams(vmem_limit_bytes=VMEM_LIMIT),
    )(*args)


def pack_amp(amp_ref, out_ref):
    across = amp_ref.shape[2] // WIDE
    parts = amp_ref.shape[1] // ROWS * across
    for d in range(parts):
        i, c = divmod(d, across)
        for tile in range(TILES):
            at = c * WIDE + tile * LANES
            part = amp_ref[:, i * ROWS : (i + 1) * ROWS, at : at + LANES]
            out_ref[d, tile] = part
            out_ref[parts + d, tile] = part


def pack_lam(where_ref, lam_ref, *out_refs):
    y = where_ref[2]
    for s, out_ref in enumerate(out_refs):
        for i in range(lam_ref.shape[1] // ROWS):
            for tile in range(TILES):
                at = pl.multiple_of((y ^ s) * WIDE + tile * LANES, LANES)
                out_ref[i, tile] = lam_ref[:, i * ROWS : (i + 1) * ROWS, pl.ds(at, LANES)]


def regroup(where_ref, *refs):
    z4 = where_ref[1]
    ins, outs = refs[:STEPS], refs[STEPS:]
    for u, out_ref in enumerate(outs):
        for s, in_ref in enumerate(ins):
            out_ref[s] = in_ref[z4 ^ u]


def unpack(parts_ref, out_ref):
    across = out_ref.shape[2] // WIDE
    for d in range(parts_ref.shape[0]):
        i, c = divmod(d, across)
        for tile in range(TILES):
            at = c * WIDE + tile * LANES
            out_ref[:, i * ROWS : (i + 1) * ROWS, at : at + LANES] = parts_ref[d, :, tile]


def swap_matrix():
    i = lax.broadcasted_iota(jnp.int32, (SIDE, SIDE), 0)
    j = lax.broadcasted_iota(jnp.int32, (SIDE, SIDE), 1)
    return (j == (i % ROWS) * ROWS + i // ROWS).astype(jnp.float32).astype(jnp.bfloat16)


def to_matrix(swap, tiles, out_ref, first):
    both = jnp.concatenate(tiles, axis=1)
    for q in range(both.shape[0] // SIDE):
        moved = jnp.dot(swap, both[q * SIDE : (q + 1) * SIDE], preferred_element_type=jnp.float32)
        moved = moved.astype(jnp.bfloat16)
        at = pl.ds(pl.multiple_of(first + q * ROWS, ROWS), ROWS)
        for s in range(ROWS):
            out_ref[at, s * WIDE : (s + 1) * WIDE] = moved[s * ROWS : (s + 1) * ROWS]


def upper_blocks(pairs):
    n = pairs // BLOCK
    return [(i, j) for i in range(n) for j in range(i, n)]


def cross_kernel(where_ref, *refs):
    lam_refs, (parts_ref, sym_ref, amp_ref, lam_ref, cross_ref) = refs[:STEPS], refs[STEPS:]
    zb, z4, y = where_ref[0], where_ref[1], where_ref[2]
    swap = swap_matrix()
    panels, _, panel_size = parts_ref.shape[:3]
    chunk = STEPS * panel_size

    def relayout(step, carry):
        tiles = [parts_ref[pl.ds(STEPS * step, STEPS), tile].reshape(chunk * ROWS, LANES) for tile in range(TILES)]
        to_matrix(swap, tiles, amp_ref, step * chunk)
        return carry

    lax.fori_loop(0, panels // STEPS, relayout, 0)
    for u, part_ref in enumerate(lam_refs):
        tiles = [
            jnp.concatenate([part_ref[y ^ k, tile].reshape(panel_size * ROWS, LANES) for k in range(STEPS)], axis=0)
            for tile in range(TILES)
        ]
        to_matrix(swap, tiles, lam_ref, (z4 ^ u) * chunk)
    half = lam_ref.shape[0]
    cross = lax.dot_general(
        lam_ref[...], amp_ref[...], (((1,), (1,)), ((), ())), preferred_element_type=jnp.float32
    )
    cross_ref[pl.ds(pl.multiple_of(zb * half, half), half)] = cross
    cross_ref[pl.ds(pl.multiple_of((1 - zb) * half, half), half)] = jnp.zeros_like(cross)
    sym = 0.5 * (cross_ref[...] + cross_ref[...].T)
    for n, (i, j) in enumerate(upper_blocks(2 * half)):
        sym_ref[n * BLOCK : (n + 1) * BLOCK] = sym[i * BLOCK : (i + 1) * BLOCK, j * BLOCK : (j + 1) * BLOCK]


def density_kernel(where_ref, upper_ref, listed_ref, amp_ref, out_ref, inter_ref, flat_ref):
    pairs, depth = amp_ref.shape
    half = flat_ref.shape[0]
    panels = listed_ref.shape[0]
    panel_size = pairs // panels
    row = lax.broadcasted_iota(jnp.int32, (pairs, panels), 0)
    first = lax.broadcasted_iota(jnp.int32, (pairs, panels), 1) * panel_size
    spread = ((row >= first) & (row < first + panel_size)).astype(jnp.float32)
    mask = jnp.dot(spread, listed_ref[...], preferred_element_type=jnp.float32)
    mask = lax.dot_general(mask, spread, (((1,), (1,)), ((), ())), preferred_element_type=jnp.float32)
    for n, (i, j) in enumerate(upper_blocks(pairs)):
        block = upper_ref[n * BLOCK : (n + 1) * BLOCK].astype(jnp.float32)
        rows, cols = slice(i * BLOCK, (i + 1) * BLOCK), slice(j * BLOCK, (j + 1) * BLOCK)
        inter_ref[rows, cols] = (block * mask[rows, cols]).astype(jnp.bfloat16)
        if i != j:
            inter_ref[cols, rows] = (block.T * mask[cols, rows]).astype(jnp.bfloat16)
    own = inter_ref[pl.ds(pl.multiple_of(where_ref[0] * half, half), half)]
    for c in range(depth // WIDE):
        flat_ref[:, c * WIDE : (c + 1) * WIDE] = jnp.dot(
            own, amp_ref[:, c * WIDE : (c + 1) * WIDE], preferred_element_type=jnp.float32
        ).astype(jnp.bfloat16)
    swap = swap_matrix()

    def relayout(step, carry):
        rows = pl.ds(pl.multiple_of(step * ROWS, ROWS), ROWS)
        both = jnp.concatenate([flat_ref[rows, s * WIDE : (s + 1) * WIDE] for s in range(ROWS)], axis=0)
        moved = jnp.dot(swap, both, preferred_element_type=jnp.float32).astype(jnp.bfloat16)
        for tile in range(TILES):
            out_ref[rows, tile] = moved[:, tile * LANES : (tile + 1) * LANES].reshape(ROWS, ROWS, LANES)
        return carry

    lax.fori_loop(0, half // ROWS, relayout, 0)


def exchange(x, axis):
    return lax.all_to_all(x, axis, split_axis=0, concat_axis=0, tiled=True)


def shifts(parts, axis):
    return [parts[0]] + [
        lax.ppermute(part, axis, [(k, k ^ s) for k in range(STEPS)]) for s, part in enumerate(parts) if s > 0
    ]


def on_device(lambda_amps, t_amps, panel_home, pair_list):
    npanels = lax.axis_size(PAIR)
    panel_size, rows, cols = lambda_amps.shape
    pairs, half = npanels * panel_size, npanels * panel_size // 2
    depth = ROWS * WIDE
    bf16, f32 = jnp.bfloat16, jnp.float32
    where = jnp.stack([lax.axis_index("zb"), lax.axis_index("z4"), lax.axis_index("y")]).astype(jnp.int32)

    home = onehot(panel_home, npanels)
    first = jnp.dot(onehot(pair_list[:, 0], npanels), home, precision=lax.Precision.HIGHEST)
    second = jnp.dot(onehot(pair_list[:, 1], npanels), home, precision=lax.Precision.HIGHEST)
    listed = jnp.dot(first.T, second, precision=lax.Precision.HIGHEST)
    listed = jnp.minimum(listed + listed.T, 1.0)

    part = (TILES, panel_size, ROWS, LANES)
    amp_parts = call(pack_amp, jax.ShapeDtypeStruct((npanels,) + part, bf16), (t_amps,))
    amp_parts = exchange(amp_parts, PAIR)
    four = [jax.ShapeDtypeStruct((STEPS,) + part, bf16)] * STEPS
    lam_parts = shifts(call(pack_lam, four, (where, lambda_amps), scalars=1), "y")
    lam_parts = shifts(call(regroup, four, (where, *lam_parts), scalars=1), "z4")
    nblocks = len(upper_blocks(pairs))
    sym, amp = call(
        cross_kernel,
        [
            jax.ShapeDtypeStruct((nblocks * BLOCK, BLOCK), f32),
            jax.ShapeDtypeStruct((pairs, depth), bf16),
        ],
        (where, *lam_parts, amp_parts),
        [pltpu.VMEM((half, depth), bf16), pltpu.VMEM((pairs, pairs), f32)],
        scalars=1,
    )
    plane, height = lax.axis_size(PLANE), lax.axis_size(LINE)
    own = nblocks * BLOCK // plane
    terms = exchange(sym.reshape(plane, own, BLOCK), PLANE)
    terms = jnp.broadcast_to(jnp.sum(terms, axis=0), (height, own, BLOCK))
    total = jnp.sum(exchange(terms, LINE), axis=0).astype(bf16)
    upper = exchange(jnp.broadcast_to(total, (plane, own, BLOCK)), PLANE)
    result = call(
        density_kernel,
        jax.ShapeDtypeStruct((half, TILES, ROWS, LANES), bf16),
        (where, upper.reshape(nblocks * BLOCK, BLOCK), listed, amp),
        [pltpu.VMEM((pairs, pairs), bf16), pltpu.VMEM((half, depth), bf16)],
        scalars=1,
    )
    result = exchange(result.reshape(npanels // 2, panel_size, TILES, ROWS, LANES), HALF)
    return call(unpack, jax.ShapeDtypeStruct(lambda_amps.shape, bf16), (result,))


def solution(mesh):
    fine = Mesh(mesh.devices.reshape(2, 4, 4, 2, 4, 2), PAIR + VIRT)
    placed = (P(PAIR, VIRT, None), P(PAIR, VIRT, None), P(), P())
    return jax.shard_map(
        on_device, mesh=fine, in_specs=placed, out_specs=P(PAIR, VIRT, None), check_vma=False
    )
```

```python
import jax
import jax.numpy as jnp
from jax import lax
from jax.experimental import pallas as pl
from jax.experimental.pallas import tpu as pltpu
from jax.sharding import Mesh, PartitionSpec as P

HALF = ("z4", "y")
PAIR = ("zb",) + HALF
VIRT = ("zh", "x", "c")
PLANE = ("y", "x", "c")
LINE = ("zb", "z4", "zh")

ROWS = 16
LANES = 128
TILES = 2
WIDE = TILES * LANES
SIDE = ROWS * ROWS
STEPS = 4
BLOCK = 128
VMEM_LIMIT = 48 * 1024 * 1024


def onehot(index, count):
    return (index[:, None] == jnp.arange(count)[None, :]).astype(jnp.float32)


def call(body, out_shape, args, scratch=(), scalars=0, free_in=(), free_out=()):
    many = isinstance(out_shape, (list, tuple))
    outs = out_shape if many else [out_shape]
    smem, vmem, free = (pl.BlockSpec(memory_space=m) for m in (pltpu.SMEM, pltpu.VMEM, pl.ANY))
    out_specs = [free if n in free_out else vmem for n in range(len(outs))]
    return pl.pallas_call(
        body,
        out_shape=out_shape,
        in_specs=[smem] * scalars + [free if n in free_in else vmem for n in range(scalars, len(args))],
        out_specs=out_specs if many else out_specs[0],
        scratch_shapes=list(scratch),
        compiler_params=pltpu.CompilerParams(vmem_limit_bytes=VMEM_LIMIT),
    )(*args)


def dma(count):
    return pltpu.SemaphoreType.DMA((count,))


def pack_amp(amp_ref, out_ref, sems):
    across = amp_ref.shape[2] // WIDE
    parts = amp_ref.shape[1] // ROWS * across
    copies = []
    for d in range(parts):
        i, c = divmod(d, across)
        for tile in range(TILES):
            at = c * WIDE + tile * LANES
            part = amp_ref.at[:, pl.ds(i * ROWS, ROWS), pl.ds(at, LANES)]
            for twin in (d, parts + d):
                copies.append(pltpu.make_async_copy(part, out_ref.at[twin, tile], sems.at[len(copies)]))
                copies[-1].start()
    for copy in copies:
        copy.wait()


def pack_lam(where_ref, lam_ref, *out_refs):
    y = where_ref[2]
    for s, out_ref in enumerate(out_refs):
        for i in range(lam_ref.shape[1] // ROWS):
            for tile in range(TILES):
                at = pl.multiple_of((y ^ s) * WIDE + tile * LANES, LANES)
                out_ref[i, tile] = lam_ref[:, i * ROWS : (i + 1) * ROWS, pl.ds(at, LANES)]


def regroup(where_ref, *refs):
    z4 = where_ref[1]
    ins, outs = refs[:STEPS], refs[STEPS:]
    for u, out_ref in enumerate(outs):
        for s, in_ref in enumerate(ins):
            out_ref[s] = in_ref[z4 ^ u]


def unpack(parts_ref, out_ref, sems):
    across = out_ref.shape[2] // WIDE
    copies = []
    for d in range(parts_ref.shape[0]):
        i, c = divmod(d, across)
        for tile in range(TILES):
            at = c * WIDE + tile * LANES
            part = out_ref.at[:, pl.ds(i * ROWS, ROWS), pl.ds(at, LANES)]
            copies.append(pltpu.make_async_copy(parts_ref.at[d, :, tile], part, sems.at[len(copies)]))
            copies[-1].start()
    for copy in copies:
        copy.wait()


def swap_matrix():
    i = lax.broadcasted_iota(jnp.int32, (SIDE, SIDE), 0)
    j = lax.broadcasted_iota(jnp.int32, (SIDE, SIDE), 1)
    return (j == (i % ROWS) * ROWS + i // ROWS).astype(jnp.float32).astype(jnp.bfloat16)


def to_matrix(swap, tiles, out_ref, first):
    both = jnp.concatenate(tiles, axis=1)
    for q in range(both.shape[0] // SIDE):
        moved = jnp.dot(swap, both[q * SIDE : (q + 1) * SIDE], preferred_element_type=jnp.float32)
        moved = moved.astype(jnp.bfloat16)
        at = pl.ds(first + q * ROWS, ROWS)
        for s in range(ROWS):
            out_ref[at, s * WIDE : (s + 1) * WIDE] = moved[s * ROWS : (s + 1) * ROWS]


def lam_kernel(where_ref, *refs):
    part_refs, (out_ref, panel_ref) = refs[:STEPS], refs[STEPS:]
    z4, y = where_ref[1], where_ref[2]
    for n, part_ref in enumerate(part_refs):
        for k in range(STEPS):
            panel_ref[((z4 ^ n) * STEPS + (y ^ k))] = part_ref[k]
    all_panels(panel_ref, out_ref)


def all_panels(parts_ref, out_ref, before=lambda step: None):
    swap = swap_matrix()
    panels, _, panel_size = parts_ref.shape[:3]
    chunk = STEPS * panel_size
    for step in range(panels // STEPS):
        before(step)
        tiles = [parts_ref[STEPS * step : STEPS * (step + 1), tile].reshape(chunk * ROWS, LANES) for tile in range(TILES)]
        to_matrix(swap, tiles, out_ref, step * chunk)


def upper_blocks(pairs):
    n = pairs // BLOCK
    return [(i, j) for i in range(n) for j in range(i, n)]


def cross_kernel(where_ref, lam_ref, parts_in, sym_ref, amp_ref, parts_ref, cross_ref, sems):
    zb = where_ref[0]
    copies = []
    for step in range(parts_ref.shape[0] // STEPS):
        some = pl.ds(step * STEPS, STEPS)
        copies.append(pltpu.make_async_copy(parts_in.at[some], parts_ref.at[some], sems.at[step]))
        copies[-1].start()
    all_panels(parts_ref, amp_ref, lambda step: copies[step].wait())
    half = lam_ref.shape[0]
    cross = lax.dot_general(
        lam_ref[...], amp_ref[...], (((1,), (1,)), ((), ())), preferred_element_type=jnp.float32
    )
    cross_ref[pl.ds(pl.multiple_of(zb * half, half), half)] = cross
    cross_ref[pl.ds(pl.multiple_of((1 - zb) * half, half), half)] = jnp.zeros_like(cross)
    sym = 0.5 * (cross_ref[...] + cross_ref[...].T)
    for n, (i, j) in enumerate(upper_blocks(2 * half)):
        sym_ref[n * BLOCK : (n + 1) * BLOCK] = sym[i * BLOCK : (i + 1) * BLOCK, j * BLOCK : (j + 1) * BLOCK]


def density_kernel(where_ref, upper_ref, listed_ref, amp_ref, out_ref, inter_ref, flat_ref):
    pairs, depth = amp_ref.shape
    half = flat_ref.shape[0]
    panels = listed_ref.shape[0]
    panel_size = pairs // panels
    row = lax.broadcasted_iota(jnp.int32, (pairs, panels), 0)
    first = lax.broadcasted_iota(jnp.int32, (pairs, panels), 1) * panel_size
    spread = ((row >= first) & (row < first + panel_size)).astype(jnp.float32)
    mask = jnp.dot(spread, listed_ref[...], preferred_element_type=jnp.float32)
    mask = lax.dot_general(mask, spread, (((1,), (1,)), ((), ())), preferred_element_type=jnp.float32)
    for n, (i, j) in enumerate(upper_blocks(pairs)):
        block = upper_ref[n * BLOCK : (n + 1) * BLOCK].astype(jnp.float32)
        rows, cols = slice(i * BLOCK, (i + 1) * BLOCK), slice(j * BLOCK, (j + 1) * BLOCK)
        inter_ref[rows, cols] = (block * mask[rows, cols]).astype(jnp.bfloat16)
        if i != j:
            inter_ref[cols, rows] = (block.T * mask[cols, rows]).astype(jnp.bfloat16)
    own = inter_ref[pl.ds(pl.multiple_of(where_ref[0] * half, half), half)]
    for c in range(depth // WIDE):
        flat_ref[:, c * WIDE : (c + 1) * WIDE] = jnp.dot(
            own, amp_ref[:, c * WIDE : (c + 1) * WIDE], preferred_element_type=jnp.float32
        ).astype(jnp.bfloat16)
    swap = swap_matrix()

    def relayout(step, carry):
        rows = pl.ds(pl.multiple_of(step * ROWS, ROWS), ROWS)
        both = jnp.concatenate([flat_ref[rows, s * WIDE : (s + 1) * WIDE] for s in range(ROWS)], axis=0)
        moved = jnp.dot(swap, both, preferred_element_type=jnp.float32).astype(jnp.bfloat16)
        for tile in range(TILES):
            out_ref[rows, tile] = moved[:, tile * LANES : (tile + 1) * LANES].reshape(ROWS, ROWS, LANES)
        return carry

    lax.fori_loop(0, half // ROWS, relayout, 0, unroll=True)


def exchange(x, axis):
    return lax.all_to_all(x, axis, split_axis=0, concat_axis=0, tiled=True)


def shifts(parts, axis):
    return [parts[0]] + [
        lax.ppermute(part, axis, [(k, k ^ s) for k in range(STEPS)]) for s, part in enumerate(parts) if s > 0
    ]


def on_device(lambda_amps, t_amps, panel_home, pair_list):
    npanels = lax.axis_size(PAIR)
    panel_size, rows, cols = lambda_amps.shape
    pairs, half = npanels * panel_size, npanels * panel_size // 2
    depth = ROWS * WIDE
    bf16, f32 = jnp.bfloat16, jnp.float32
    where = jnp.stack([lax.axis_index("zb"), lax.axis_index("z4"), lax.axis_index("y")]).astype(jnp.int32)

    home = onehot(panel_home, npanels)
    first = jnp.dot(onehot(pair_list[:, 0], npanels), home, precision=lax.Precision.HIGHEST)
    second = jnp.dot(onehot(pair_list[:, 1], npanels), home, precision=lax.Precision.HIGHEST)
    listed = jnp.dot(first.T, second, precision=lax.Precision.HIGHEST)
    listed = jnp.minimum(listed + listed.T, 1.0)

    part = (TILES, panel_size, ROWS, LANES)
    amp_parts = call(pack_amp, jax.ShapeDtypeStruct((npanels,) + part, bf16), (t_amps,), [dma(2 * npanels)], free_in=(0,), free_out=(0,))
    four = [jax.ShapeDtypeStruct((STEPS,) + part, bf16)] * STEPS
    lam_parts = call(pack_lam, four, (where, lambda_amps), scalars=1)
    amp_parts = exchange(amp_parts, PAIR)
    lam_parts = call(regroup, four, (where, *shifts(lam_parts, "y")), scalars=1)
    lam = call(
        lam_kernel,
        jax.ShapeDtypeStruct((half, depth), bf16),
        (where, *shifts(lam_parts, "z4")),
        [pltpu.VMEM((npanels // 2,) + part, bf16)],
        scalars=1,
    )
    nblocks = len(upper_blocks(pairs))
    sym, amp = call(
        cross_kernel,
        [
            jax.ShapeDtypeStruct((nblocks * BLOCK, BLOCK), f32),
            jax.ShapeDtypeStruct((pairs, depth), bf16),
        ],
        (where, lam, amp_parts),
        [pltpu.VMEM((npanels,) + part, bf16), pltpu.VMEM((pairs, pairs), f32), dma(npanels // STEPS)],
        scalars=1,
        free_in=(2,),
    )
    plane, height = lax.axis_size(PLANE), lax.axis_size(LINE)
    own = nblocks * BLOCK // plane
    terms = exchange(sym.reshape(plane, own, BLOCK), PLANE)
    terms = jnp.broadcast_to(jnp.sum(terms, axis=0), (height, own, BLOCK))
    total = jnp.sum(exchange(terms, LINE), axis=0).astype(bf16)
    upper = exchange(jnp.broadcast_to(total, (plane, own, BLOCK)), PLANE)
    result = call(
        density_kernel,
        jax.ShapeDtypeStruct((half, TILES, ROWS, LANES), bf16),
        (where, upper.reshape(nblocks * BLOCK, BLOCK), listed, amp),
        [pltpu.VMEM((pairs, pairs), bf16), pltpu.VMEM((half, depth), bf16)],
        scalars=1,
    )
    result = exchange(result.reshape(npanels // 2, panel_size, TILES, ROWS, LANES), HALF)
    return call(
        unpack, jax.ShapeDtypeStruct(lambda_amps.shape, bf16), (result,), [dma(npanels)], free_in=(0,), free_out=(0,)
    )


def solution(mesh):
    fine = Mesh(mesh.devices.reshape(2, 4, 4, 2, 4, 2), PAIR + VIRT)
    placed = (P(PAIR, VIRT, None), P(PAIR, VIRT, None), P(), P())
    return jax.shard_map(
        on_device, mesh=fine, in_specs=placed, out_specs=P(PAIR, VIRT, None), check_vma=False
    )
```

```python
import jax
import jax.numpy as jnp
from jax import lax
from jax.experimental import pallas as pl
from jax.experimental.pallas import tpu as pltpu
from jax.sharding import Mesh, PartitionSpec as P

HALF = ("z4", "y")
PAIR = ("zb",) + HALF
VIRT = ("zh", "x", "c")
PLANE = ("y", "x", "c")
LINE = ("zb", "z4", "zh")

ROWS = 16
LANES = 128
TILES = 2
WIDE = TILES * LANES
SIDE = ROWS * ROWS
STEPS = 4
SQUARE = 256
VMEM_LIMIT = 48 * 1024 * 1024


def onehot(index, count):
    return (index[:, None] == jnp.arange(count)[None, :]).astype(jnp.float32)


def call(body, out_shape, args, scratch=(), scalars=0, free_in=(), free_out=()):
    many = isinstance(out_shape, (list, tuple))
    outs = out_shape if many else [out_shape]
    smem, vmem, free = (pl.BlockSpec(memory_space=m) for m in (pltpu.SMEM, pltpu.VMEM, pl.ANY))
    out_specs = [free if n in free_out else vmem for n in range(len(outs))]
    return pl.pallas_call(
        body,
        out_shape=out_shape,
        in_specs=[smem] * scalars + [free if n in free_in else vmem for n in range(scalars, len(args))],
        out_specs=out_specs if many else out_specs[0],
        scratch_shapes=list(scratch),
        compiler_params=pltpu.CompilerParams(vmem_limit_bytes=VMEM_LIMIT),
    )(*args)


def dma(count):
    return pltpu.SemaphoreType.DMA((count,))


def pack_amp(amp_ref, out_ref, sems):
    across = amp_ref.shape[2] // WIDE
    parts = amp_ref.shape[1] // ROWS * across
    copies = []
    for d in range(parts):
        i, c = divmod(d, across)
        for tile in range(TILES):
            at = c * WIDE + tile * LANES
            part = amp_ref.at[:, pl.ds(i * ROWS, ROWS), pl.ds(at, LANES)]
            for twin in (d, parts + d):
                copies.append(pltpu.make_async_copy(part, out_ref.at[twin, tile], sems.at[len(copies)]))
                copies[-1].start()
    for copy in copies:
        copy.wait()


def pack_lam(where_ref, lam_ref, *out_refs):
    y = where_ref[2]
    for s, out_ref in enumerate(out_refs):
        for i in range(lam_ref.shape[1] // ROWS):
            for tile in range(TILES):
                at = pl.multiple_of((y ^ s) * WIDE + tile * LANES, LANES)
                out_ref[i, tile] = lam_ref[:, i * ROWS : (i + 1) * ROWS, pl.ds(at, LANES)]


def regroup(where_ref, *refs):
    z4 = where_ref[1]
    ins, outs = refs[:STEPS], refs[STEPS:]
    for u, out_ref in enumerate(outs):
        for s, in_ref in enumerate(ins):
            out_ref[s] = in_ref[z4 ^ u]


def unpack(parts_ref, out_ref, sems):
    across = out_ref.shape[2] // WIDE
    copies = []
    for d in range(parts_ref.shape[0]):
        i, c = divmod(d, across)
        for tile in range(TILES):
            at = c * WIDE + tile * LANES
            part = out_ref.at[:, pl.ds(i * ROWS, ROWS), pl.ds(at, LANES)]
            copies.append(pltpu.make_async_copy(parts_ref.at[d, :, tile], part, sems.at[len(copies)]))
            copies[-1].start()
    for copy in copies:
        copy.wait()


def swap_matrix():
    i = lax.broadcasted_iota(jnp.int32, (SIDE, SIDE), 0)
    j = lax.broadcasted_iota(jnp.int32, (SIDE, SIDE), 1)
    return (j == (i % ROWS) * ROWS + i // ROWS).astype(jnp.float32).astype(jnp.bfloat16)


def to_matrix(swap, tiles, out_ref, first):
    both = jnp.concatenate(tiles, axis=1)
    for q in range(both.shape[0] // SIDE):
        moved = jnp.dot(swap, both[q * SIDE : (q + 1) * SIDE], preferred_element_type=jnp.float32)
        moved = moved.astype(jnp.bfloat16)
        at = pl.ds(first + q * ROWS, ROWS)
        for s in range(ROWS):
            out_ref[at, s * WIDE : (s + 1) * WIDE] = moved[s * ROWS : (s + 1) * ROWS]


def lam_kernel(where_ref, *refs):
    part_refs, (out_ref, panel_ref) = refs[:STEPS], refs[STEPS:]
    z4, y = where_ref[1], where_ref[2]
    for n, part_ref in enumerate(part_refs):
        for k in range(STEPS):
            panel_ref[((z4 ^ n) * STEPS + (y ^ k))] = part_ref[k]
    all_panels(panel_ref, out_ref)


def all_panels(parts_ref, out_ref, before=lambda step: None):
    swap = swap_matrix()
    panels, _, panel_size = parts_ref.shape[:3]
    chunk = STEPS * panel_size
    for step in range(panels // STEPS):
        before(step)
        tiles = [parts_ref[STEPS * step : STEPS * (step + 1), tile].reshape(chunk * ROWS, LANES) for tile in range(TILES)]
        to_matrix(swap, tiles, out_ref, step * chunk)


def left_half(shape):
    return lax.broadcasted_iota(jnp.int32, shape, 1) < LANES // 2


def fold(x):
    n = x.shape[0] // 2
    return jnp.where(left_half((n, LANES)), x[:n], pltpu.roll(x[n:], LANES // 2, 1))


def unfold(x):
    return jnp.concatenate([x, pltpu.roll(x, LANES // 2, 1)], axis=0)


def cross_kernel(where_ref, lam_ref, parts_in, sym_ref, amp_ref, parts_ref, cross_ref, sems):
    zb = where_ref[0]
    copies = []
    for step in range(parts_ref.shape[0] // STEPS):
        some = pl.ds(step * STEPS, STEPS)
        copies.append(pltpu.make_async_copy(parts_in.at[some], parts_ref.at[some], sems.at[step]))
        copies[-1].start()
    all_panels(parts_ref, amp_ref, lambda step: copies[step].wait())
    half = lam_ref.shape[0]
    cross_ref[...] = jnp.zeros_like(cross_ref)
    for n, which in enumerate((zb, 1 - zb)):
        amp = amp_ref[pl.ds(pl.multiple_of(which * half, half), half)]
        cross_ref[n, :half, :half] = lax.dot_general(
            lam_ref[...], amp, (((1,), (1,)), ((), ())), preferred_element_type=jnp.float32
        )
    within, between = cross_ref[0], cross_ref[1]
    within = 0.5 * (within + within.T)
    between = 0.5 * jnp.where(zb == 0, between, between.T)
    at = 0
    for rows in (
        between[:half, :LANES],
        fold(between[:half, LANES:]),
        within[:LANES, :LANES],
        fold(within[:LANES, LANES:]),
        fold(within[LANES:half, LANES:]),
    ):
        sym_ref[at : at + rows.shape[0]] = rows
        at += rows.shape[0]


def density_kernel(where_ref, sym_ref, listed_ref, amp_ref, out_ref, square_ref, inter_ref, flat_ref):
    pairs, depth = amp_ref.shape
    half = flat_ref.shape[0]
    panels = listed_ref.shape[0]
    panel_size = pairs // panels
    zb = where_ref[0]

    def spread(first_row, rows):
        row = first_row + lax.broadcasted_iota(jnp.int32, (rows, panels), 0)
        first = lax.broadcasted_iota(jnp.int32, (rows, panels), 1) * panel_size
        return ((row >= first) & (row < first + panel_size)).astype(jnp.float32)

    mask = jnp.dot(spread(zb * half, half), listed_ref[...], preferred_element_type=jnp.float32)
    mask = lax.dot_general(mask, spread(0, pairs), (((1,), (1,)), ((), ())), preferred_element_type=jnp.float32)

    sizes = [half, half // 2, LANES, LANES // 2, (half - LANES) // 2]
    ends = [sum(sizes[: n + 1]) for n in range(len(sizes))]
    x, x_right, w, w_right, w_last = (sym_ref[e - n : e].astype(jnp.float32) for e, n in zip(ends, sizes))
    square_ref[...] = jnp.zeros_like(square_ref)
    square_ref[:half, :LANES] = x
    square_ref[:half, LANES:] = unfold(x_right)
    between = jnp.where(zb == 0, square_ref[...], square_ref[...].T)[:half]
    w_right = unfold(w_right)
    square_ref[:LANES, :LANES] = w
    square_ref[:LANES, LANES:] = w_right
    square_ref[LANES:half, :LANES] = w_right.T[: half - LANES]
    square_ref[LANES:half, LANES:] = unfold(w_last)
    within = square_ref[:half]
    left = jnp.where(zb == 0, within, between)
    right = jnp.where(zb == 0, between, within)
    keep = left_half((half, LANES))
    turned = [pltpu.roll(right[:, n * LANES : (n + 1) * LANES], LANES // 2, 1) for n in range(2)]
    for n, block in enumerate(
        (left[:, :LANES], jnp.where(keep, left[:, LANES:], turned[0]), jnp.where(keep, turned[0], turned[1]))
    ):
        cols = slice(n * LANES, (n + 1) * LANES)
        inter_ref[:, cols] = (block * mask[:, cols]).astype(jnp.bfloat16)
    own = inter_ref[...]
    for c in range(depth // WIDE):
        flat_ref[:, c * WIDE : (c + 1) * WIDE] = jnp.dot(
            own, amp_ref[:, c * WIDE : (c + 1) * WIDE], preferred_element_type=jnp.float32
        ).astype(jnp.bfloat16)
    swap = swap_matrix()

    def relayout(step, carry):
        rows = pl.ds(pl.multiple_of(step * ROWS, ROWS), ROWS)
        both = jnp.concatenate([flat_ref[rows, s * WIDE : (s + 1) * WIDE] for s in range(ROWS)], axis=0)
        moved = jnp.dot(swap, both, preferred_element_type=jnp.float32).astype(jnp.bfloat16)
        for tile in range(TILES):
            out_ref[rows, tile] = moved[:, tile * LANES : (tile + 1) * LANES].reshape(ROWS, ROWS, LANES)
        return carry

    lax.fori_loop(0, half // ROWS, relayout, 0, unroll=True)


def exchange(x, axis):
    return lax.all_to_all(x, axis, split_axis=0, concat_axis=0, tiled=True)


def shifts(parts, axis):
    return [parts[0]] + [
        lax.ppermute(part, axis, [(k, k ^ s) for k in range(STEPS)]) for s, part in enumerate(parts) if s > 0
    ]


def on_device(lambda_amps, t_amps, panel_home, pair_list):
    npanels = lax.axis_size(PAIR)
    panel_size, rows, cols = lambda_amps.shape
    pairs, half = npanels * panel_size, npanels * panel_size // 2
    depth = ROWS * WIDE
    folded = half + half // 2 + LANES + LANES // 2 + (half - LANES) // 2
    bf16, f32 = jnp.bfloat16, jnp.float32
    where = jnp.stack([lax.axis_index("zb"), lax.axis_index("z4"), lax.axis_index("y")]).astype(jnp.int32)

    home = onehot(panel_home, npanels)
    first = jnp.dot(onehot(pair_list[:, 0], npanels), home, precision=lax.Precision.HIGHEST)
    second = jnp.dot(onehot(pair_list[:, 1], npanels), home, precision=lax.Precision.HIGHEST)
    listed = jnp.dot(first.T, second, precision=lax.Precision.HIGHEST)
    listed = jnp.minimum(listed + listed.T, 1.0)

    part = (TILES, panel_size, ROWS, LANES)
    amp_parts = call(pack_amp, jax.ShapeDtypeStruct((npanels,) + part, bf16), (t_amps,), [dma(2 * npanels)], free_in=(0,), free_out=(0,))
    four = [jax.ShapeDtypeStruct((STEPS,) + part, bf16)] * STEPS
    lam_parts = call(pack_lam, four, (where, lambda_amps), scalars=1)
    amp_parts = exchange(amp_parts, PAIR)
    lam_parts = call(regroup, four, (where, *shifts(lam_parts, "y")), scalars=1)
    lam = call(
        lam_kernel,
        jax.ShapeDtypeStruct((half, depth), bf16),
        (where, *shifts(lam_parts, "z4")),
        [pltpu.VMEM((npanels // 2,) + part, bf16)],
        scalars=1,
    )
    sym, amp = call(
        cross_kernel,
        [
            jax.ShapeDtypeStruct((folded, LANES), f32),
            jax.ShapeDtypeStruct((pairs, depth), bf16),
        ],
        (where, lam, amp_parts),
        [pltpu.VMEM((npanels,) + part, bf16), pltpu.VMEM((2, SQUARE, SQUARE), f32), dma(npanels // STEPS)],
        scalars=1,
        free_in=(2,),
    )
    plane, height = lax.axis_size(PLANE), lax.axis_size(LINE)
    own = folded // plane
    terms = exchange(sym.reshape(plane, own, LANES), PLANE)
    terms = exchange(jnp.broadcast_to(jnp.sum(terms, axis=0), (height, own, LANES)), LINE)
    halves = terms.reshape(2, height // 2, own, LANES).sum(axis=1)
    mine = jnp.where(where[0] == 0, halves[0], halves[1])
    both = lax.axis_index(PLANE) * own < half * half // LANES
    total = jnp.where(both, halves[0] + halves[1], mine).astype(bf16)
    upper = exchange(jnp.broadcast_to(total, (plane, own, LANES)), PLANE)
    result = call(
        density_kernel,
        jax.ShapeDtypeStruct((half, TILES, ROWS, LANES), bf16),
        (where, upper.reshape(folded, LANES), listed, amp),
        [pltpu.VMEM((SQUARE, SQUARE), f32), pltpu.VMEM((half, pairs), bf16), pltpu.VMEM((half, depth), bf16)],
        scalars=1,
    )
    result = exchange(result.reshape(npanels // 2, panel_size, TILES, ROWS, LANES), HALF)
    return call(
        unpack, jax.ShapeDtypeStruct(lambda_amps.shape, bf16), (result,), [dma(npanels)], free_in=(0,), free_out=(0,)
    )


def solution(mesh):
    fine = Mesh(mesh.devices.reshape(2, 4, 4, 2, 4, 2), PAIR + VIRT)
    placed = (P(PAIR, VIRT, None), P(PAIR, VIRT, None), P(), P())
    return jax.shard_map(
        on_device, mesh=fine, in_specs=placed, out_specs=P(PAIR, VIRT, None), check_vma=False
    )
```

```python
import jax
import jax.numpy as jnp
from jax import lax
from jax.experimental import pallas as pl
from jax.experimental.pallas import tpu as pltpu
from jax.sharding import Mesh, PartitionSpec as P

HALF = ("z4", "y")
PAIR = ("zb",) + HALF
VIRT = ("zh", "x", "c")
PLANE = ("y", "x", "c")
LINE = ("zb", "z4", "zh")

ROWS = 16
LANES = 128
TILES = 2
WIDE = TILES * LANES
SIDE = ROWS * ROWS
STEPS = 4
SQUARE = 256
VMEM_LIMIT = 48 * 1024 * 1024
VMEM_MOST = 62 * 1024 * 1024


def onehot(index, count):
    return (index[:, None] == jnp.arange(count)[None, :]).astype(jnp.float32)


def call(body, out_shape, args, scratch=(), scalars=0, free_in=(), free_out=(), limit=VMEM_LIMIT):
    many = isinstance(out_shape, (list, tuple))
    outs = out_shape if many else [out_shape]
    smem, vmem, free = (pl.BlockSpec(memory_space=m) for m in (pltpu.SMEM, pltpu.VMEM, pl.ANY))
    out_specs = [free if n in free_out else vmem for n in range(len(outs))]
    return pl.pallas_call(
        body,
        out_shape=out_shape,
        in_specs=[smem] * scalars + [free if n in free_in else vmem for n in range(scalars, len(args))],
        out_specs=out_specs if many else out_specs[0],
        scratch_shapes=list(scratch),
        compiler_params=pltpu.CompilerParams(vmem_limit_bytes=limit),
    )(*args)


def dma(count):
    return pltpu.SemaphoreType.DMA((count,))


def pack_amp(amp_ref, out_ref, sems):
    across = amp_ref.shape[2] // WIDE
    parts = amp_ref.shape[1] // ROWS * across
    copies = []
    for d in range(parts):
        i, c = divmod(d, across)
        for tile in range(TILES):
            at = c * WIDE + tile * LANES
            part = amp_ref.at[:, pl.ds(i * ROWS, ROWS), pl.ds(at, LANES)]
            for twin in (d, parts + d):
                copies.append(pltpu.make_async_copy(part, out_ref.at[twin, tile], sems.at[len(copies)]))
                copies[-1].start()
    for copy in copies:
        copy.wait()


def pack_lam(where_ref, lam_ref, *out_refs):
    y = where_ref[2]
    for s, out_ref in enumerate(out_refs):
        for i in range(lam_ref.shape[1] // ROWS):
            for tile in range(TILES):
                at = pl.multiple_of((y ^ s) * WIDE + tile * LANES, LANES)
                out_ref[i, tile] = lam_ref[:, i * ROWS : (i + 1) * ROWS, pl.ds(at, LANES)]


def regroup(where_ref, *refs):
    z4 = where_ref[1]
    ins, outs = refs[:STEPS], refs[STEPS:]
    for u, out_ref in enumerate(outs):
        for s, in_ref in enumerate(ins):
            out_ref[s] = in_ref[z4 ^ u]


def unpack(parts_ref, out_ref, sems):
    across = out_ref.shape[2] // WIDE
    copies = []
    for d in range(parts_ref.shape[0]):
        i, c = divmod(d, across)
        for tile in range(TILES):
            at = c * WIDE + tile * LANES
            part = out_ref.at[:, pl.ds(i * ROWS, ROWS), pl.ds(at, LANES)]
            copies.append(pltpu.make_async_copy(parts_ref.at[d, :, tile], part, sems.at[len(copies)]))
            copies[-1].start()
    for copy in copies:
        copy.wait()


def swap_matrix():
    i = lax.broadcasted_iota(jnp.int32, (SIDE, SIDE), 0)
    j = lax.broadcasted_iota(jnp.int32, (SIDE, SIDE), 1)
    return (j == (i % ROWS) * ROWS + i // ROWS).astype(jnp.float32).astype(jnp.bfloat16)


def to_matrix(swap, tiles, out_ref, first):
    both = jnp.concatenate(tiles, axis=1)
    for q in range(both.shape[0] // SIDE):
        moved = jnp.dot(swap, both[q * SIDE : (q + 1) * SIDE], preferred_element_type=jnp.float32)
        moved = moved.astype(jnp.bfloat16)
        at = pl.ds(first + q * ROWS, ROWS)
        for s in range(ROWS):
            out_ref[at, s * WIDE : (s + 1) * WIDE] = moved[s * ROWS : (s + 1) * ROWS]


def lam_kernel(where_ref, *refs):
    part_refs, (out_ref, panel_ref) = refs[:STEPS], refs[STEPS:]
    z4, y = where_ref[1], where_ref[2]
    for n, part_ref in enumerate(part_refs):
        for k in range(STEPS):
            panel_ref[((z4 ^ n) * STEPS + (y ^ k))] = part_ref[k]
    all_panels(panel_ref, out_ref)


def all_panels(parts_ref, out_ref, before=lambda step: None):
    swap = swap_matrix()
    panels, _, panel_size = parts_ref.shape[:3]
    chunk = STEPS * panel_size
    for step in range(panels // STEPS):
        before(step)
        tiles = [parts_ref[STEPS * step : STEPS * (step + 1), tile].reshape(chunk * ROWS, LANES) for tile in range(TILES)]
        to_matrix(swap, tiles, out_ref, step * chunk)


def left_half(shape):
    return lax.broadcasted_iota(jnp.int32, shape, 1) < LANES // 2


def fold(x):
    n = x.shape[0] // 2
    return jnp.where(left_half((n, LANES)), x[:n], pltpu.roll(x[n:], LANES // 2, 1))


def unfold(x):
    return jnp.concatenate([x, pltpu.roll(x, LANES // 2, 1)], axis=0)


def amp_kernel(parts_in, amp_ref, parts_ref, sems):
    copies = []
    for step in range(parts_ref.shape[0] // STEPS):
        some = pl.ds(step * STEPS, STEPS)
        copies.append(pltpu.make_async_copy(parts_in.at[some], parts_ref.at[some], sems.at[step]))
        copies[-1].start()
    all_panels(parts_ref, amp_ref, lambda step: copies[step].wait())


def cross_kernel(where_ref, lam_in, parts_ref, sym_ref, lam_ref, amp_ref, cross_ref, sem):
    zb = where_ref[0]
    come = pltpu.make_async_copy(lam_in, lam_ref, sem.at[0])
    come.start()
    all_panels(parts_ref, amp_ref)
    come.wait()
    half = lam_ref.shape[0]
    cross_ref[...] = jnp.zeros_like(cross_ref)
    for n, which in enumerate((zb, 1 - zb)):
        amp = amp_ref[pl.ds(pl.multiple_of(which * half, half), half)]
        cross_ref[n, :half, :half] = lax.dot_general(
            lam_ref[...], amp, (((1,), (1,)), ((), ())), preferred_element_type=jnp.float32
        )
    within, between = cross_ref[0], cross_ref[1]
    within = 0.5 * (within + within.T)
    between = 0.5 * jnp.where(zb == 0, between, between.T)
    at = 0
    for rows in (
        between[:half, :LANES],
        fold(between[:half, LANES:]),
        within[:LANES, :LANES],
        fold(within[:LANES, LANES:]),
        fold(within[LANES:half, LANES:]),
    ):
        sym_ref[at : at + rows.shape[0]] = rows
        at += rows.shape[0]


def first_sum(terms_ref, out_ref):
    out_ref[...] = jnp.broadcast_to(jnp.sum(terms_ref[...], axis=0), out_ref.shape)


def second_sum(where_ref, terms_ref, out_ref):
    height = terms_ref.shape[0]
    halves = [jnp.sum(terms_ref[n * height // 2 : (n + 1) * height // 2], axis=0) for n in range(2)]
    mine = jnp.where(where_ref[0] == 0, halves[0], halves[1])
    total = jnp.where(where_ref[3] == 1, halves[0] + halves[1], mine).astype(jnp.bfloat16)
    out_ref[...] = jnp.broadcast_to(total, out_ref.shape)


def density_kernel(where_ref, sym_ref, listed_ref, amp_ref, out_ref, square_ref, inter_ref, flat_ref):
    pairs, depth = amp_ref.shape
    half = flat_ref.shape[0]
    panels = listed_ref.shape[0]
    panel_size = pairs // panels
    zb = where_ref[0]

    def spread(first_row, rows):
        row = first_row + lax.broadcasted_iota(jnp.int32, (rows, panels), 0)
        first = lax.broadcasted_iota(jnp.int32, (rows, panels), 1) * panel_size
        return ((row >= first) & (row < first + panel_size)).astype(jnp.float32)

    mask = jnp.dot(spread(zb * half, half), listed_ref[...], preferred_element_type=jnp.float32)
    mask = lax.dot_general(mask, spread(0, pairs), (((1,), (1,)), ((), ())), preferred_element_type=jnp.float32)

    sizes = [half, half // 2, LANES, LANES // 2, (half - LANES) // 2]
    ends = [sum(sizes[: n + 1]) for n in range(len(sizes))]
    x, x_right, w, w_right, w_last = (sym_ref[e - n : e].astype(jnp.float32) for e, n in zip(ends, sizes))
    square_ref[...] = jnp.zeros_like(square_ref)
    square_ref[:half, :LANES] = x
    square_ref[:half, LANES:] = unfold(x_right)
    between = jnp.where(zb == 0, square_ref[...], square_ref[...].T)[:half]
    w_right = unfold(w_right)
    square_ref[:LANES, :LANES] = w
    square_ref[:LANES, LANES:] = w_right
    square_ref[LANES:half, :LANES] = w_right.T[: half - LANES]
    square_ref[LANES:half, LANES:] = unfold(w_last)
    within = square_ref[:half]
    left = jnp.where(zb == 0, within, between)
    right = jnp.where(zb == 0, between, within)
    keep = left_half((half, LANES))
    turned = [pltpu.roll(right[:, n * LANES : (n + 1) * LANES], LANES // 2, 1) for n in range(2)]
    for n, block in enumerate(
        (left[:, :LANES], jnp.where(keep, left[:, LANES:], turned[0]), jnp.where(keep, turned[0], turned[1]))
    ):
        cols = slice(n * LANES, (n + 1) * LANES)
        inter_ref[:, cols] = (block * mask[:, cols]).astype(jnp.bfloat16)
    own = inter_ref[...]
    for c in range(depth // WIDE):
        flat_ref[:, c * WIDE : (c + 1) * WIDE] = jnp.dot(
            own, amp_ref[:, c * WIDE : (c + 1) * WIDE], preferred_element_type=jnp.float32
        ).astype(jnp.bfloat16)
    swap = swap_matrix()

    def relayout(step, carry):
        rows = pl.ds(pl.multiple_of(step * ROWS, ROWS), ROWS)
        both = jnp.concatenate([flat_ref[rows, s * WIDE : (s + 1) * WIDE] for s in range(ROWS)], axis=0)
        moved = jnp.dot(swap, both, preferred_element_type=jnp.float32).astype(jnp.bfloat16)
        for tile in range(TILES):
            out_ref[rows, tile] = moved[:, tile * LANES : (tile + 1) * LANES].reshape(ROWS, ROWS, LANES)
        return carry

    lax.fori_loop(0, half // ROWS, relayout, 0, unroll=True)


def exchange(x, axis):
    return lax.all_to_all(x, axis, split_axis=0, concat_axis=0, tiled=True)


def shifts(parts, axis):
    return [parts[0]] + [
        lax.ppermute(part, axis, [(k, k ^ s) for k in range(STEPS)]) for s, part in enumerate(parts) if s > 0
    ]


def on_device(lambda_amps, t_amps, panel_home, pair_list):
    npanels = lax.axis_size(PAIR)
    panel_size, rows, cols = lambda_amps.shape
    pairs, half = npanels * panel_size, npanels * panel_size // 2
    depth = ROWS * WIDE
    bf16, f32 = jnp.bfloat16, jnp.float32
    folded = half + half // 2 + LANES + LANES // 2 + (half - LANES) // 2
    plane, height = lax.axis_size(PLANE), lax.axis_size(LINE)
    own = folded // plane
    between = lax.axis_index(PLANE) * own < half * half // LANES
    where = [lax.axis_index("zb"), lax.axis_index("z4"), lax.axis_index("y"), between]
    where = jnp.stack([w.astype(jnp.int32) for w in where])

    home = onehot(panel_home, npanels)
    first = jnp.dot(onehot(pair_list[:, 0], npanels), home, precision=lax.Precision.HIGHEST)
    second = jnp.dot(onehot(pair_list[:, 1], npanels), home, precision=lax.Precision.HIGHEST)
    listed = jnp.dot(first.T, second, precision=lax.Precision.HIGHEST)
    listed = jnp.minimum(listed + listed.T, 1.0)

    part = (TILES, panel_size, ROWS, LANES)
    amp_parts = call(pack_amp, jax.ShapeDtypeStruct((npanels,) + part, bf16), (t_amps,), [dma(2 * npanels)], free_out=(0,), limit=VMEM_MOST)
    four = [jax.ShapeDtypeStruct((STEPS,) + part, bf16)] * STEPS
    lam_parts = call(pack_lam, four, (where, lambda_amps), scalars=1)
    amp_parts = exchange(amp_parts, PAIR)
    lam_parts = call(regroup, four, (where, *shifts(lam_parts, "y")), scalars=1)
    lam = call(
        lam_kernel,
        jax.ShapeDtypeStruct((half, depth), bf16),
        (where, *shifts(lam_parts, "z4")),
        [pltpu.VMEM((npanels // 2,) + part, bf16)],
        scalars=1,
    )
    brought = [pltpu.VMEM((npanels,) + part, bf16), dma(npanels // STEPS)]
    sym = call(
        cross_kernel,
        jax.ShapeDtypeStruct((folded, LANES), f32),
        (where, lam, amp_parts),
        [
            pltpu.VMEM((half, depth), bf16),
            pltpu.VMEM((pairs, depth), bf16),
            pltpu.VMEM((2, SQUARE, SQUARE), f32),
            dma(1),
        ],
        scalars=1,
        free_in=(1,),
        limit=VMEM_LIMIT,
    )
    terms = exchange(sym.reshape(plane, own, LANES), PLANE)
    terms = call(first_sum, jax.ShapeDtypeStruct((height, own, LANES), f32), (terms,))
    terms = exchange(terms, LINE)
    terms = call(second_sum, jax.ShapeDtypeStruct((plane, own, LANES), bf16), (where, terms), scalars=1)
    later, _ = lax.optimization_barrier((amp_parts, terms))
    upper = exchange(terms, PLANE)
    amp = call(amp_kernel, jax.ShapeDtypeStruct((pairs, depth), bf16), (later,), brought, free_in=(0,))
    result = call(
        density_kernel,
        jax.ShapeDtypeStruct((half, TILES, ROWS, LANES), bf16),
        (where, upper.reshape(folded, LANES), listed, amp),
        [pltpu.VMEM((SQUARE, SQUARE), f32), pltpu.VMEM((half, pairs), bf16), pltpu.VMEM((half, depth), bf16)],
        scalars=1,
    )
    result = exchange(result.reshape(npanels // 2, panel_size, TILES, ROWS, LANES), HALF)
    return call(
        unpack, jax.ShapeDtypeStruct(lambda_amps.shape, bf16), (result,), [dma(npanels)], free_in=(0,), free_out=(0,)
    )


def solution(mesh):
    fine = Mesh(mesh.devices.reshape(2, 4, 4, 2, 4, 2), PAIR + VIRT)
    placed = (P(PAIR, VIRT, None), P(PAIR, VIRT, None), P(), P())
    return jax.shard_map(
        on_device, mesh=fine, in_specs=placed, out_specs=P(PAIR, VIRT, None), check_vma=False
    )
```

```python
import jax
import jax.numpy as jnp
from jax import lax
from jax.experimental import pallas as pl
from jax.experimental.pallas import tpu as pltpu
from jax.sharding import Mesh, PartitionSpec as P

HALF = ("z4", "y")
PAIR = ("zb",) + HALF
VIRT = ("zh", "x", "c")
PLANE = ("y", "x", "c")
LINE = ("zb", "z4", "zh")

ROWS = 16
LANES = 128
TILES = 2
WIDE = TILES * LANES
SIDE = ROWS * ROWS
STEPS = 4
SQUARE = 256
VMEM_LIMIT = 48 * 1024 * 1024
VMEM_MOST = 62 * 1024 * 1024


def onehot(index, count):
    return (index[:, None] == jnp.arange(count)[None, :]).astype(jnp.float32)


def call(body, out_shape, args, scratch=(), scalars=0, free_in=(), free_out=(), limit=VMEM_LIMIT):
    many = isinstance(out_shape, (list, tuple))
    outs = out_shape if many else [out_shape]
    smem, vmem, free = (pl.BlockSpec(memory_space=m) for m in (pltpu.SMEM, pltpu.VMEM, pl.ANY))
    out_specs = [free if n in free_out else vmem for n in range(len(outs))]
    return pl.pallas_call(
        body,
        out_shape=out_shape,
        in_specs=[smem] * scalars + [free if n in free_in else vmem for n in range(scalars, len(args))],
        out_specs=out_specs if many else out_specs[0],
        scratch_shapes=list(scratch),
        compiler_params=pltpu.CompilerParams(vmem_limit_bytes=limit),
    )(*args)


def dma(count):
    return pltpu.SemaphoreType.DMA((count,))


def pack_amp(amp_in, out_ref, amp_ref, sems):
    across = amp_ref.shape[2] // WIDE
    down = amp_ref.shape[1] // ROWS
    come, go = [], []
    for i in range(down):
        rows = (slice(None), pl.ds(i * ROWS, ROWS))
        come.append(pltpu.make_async_copy(amp_in.at[rows], amp_ref.at[rows], sems.at[i]))
        come[-1].start()
    for i in range(down):
        come[i].wait()
        for c in range(across):
            for tile in range(TILES):
                part = amp_ref.at[:, pl.ds(i * ROWS, ROWS), pl.ds(c * WIDE + tile * LANES, LANES)]
                for twin in range(2):
                    place = out_ref.at[(twin * down + i) * across + c, tile]
                    go.append(pltpu.make_async_copy(part, place, sems.at[down + len(go)]))
                    go[-1].start()
    for copy in go:
        copy.wait()


def pack_lam(where_ref, lam_ref, *out_refs):
    y = where_ref[2]
    for s, out_ref in enumerate(out_refs):
        for i in range(lam_ref.shape[1] // ROWS):
            for tile in range(TILES):
                at = pl.multiple_of((y ^ s) * WIDE + tile * LANES, LANES)
                out_ref[i, tile] = lam_ref[:, i * ROWS : (i + 1) * ROWS, pl.ds(at, LANES)]


def regroup(where_ref, *refs):
    z4 = where_ref[1]
    ins, outs = refs[:STEPS], refs[STEPS:]
    for u, out_ref in enumerate(outs):
        for s, in_ref in enumerate(ins):
            out_ref[s] = in_ref[z4 ^ u]


def unpack(parts_ref, out_ref, sems):
    across = out_ref.shape[2] // WIDE
    copies = []
    for d in range(parts_ref.shape[0]):
        i, c = divmod(d, across)
        for tile in range(TILES):
            at = c * WIDE + tile * LANES
            part = out_ref.at[:, pl.ds(i * ROWS, ROWS), pl.ds(at, LANES)]
            copies.append(pltpu.make_async_copy(parts_ref.at[d, :, tile], part, sems.at[len(copies)]))
            copies[-1].start()
    for copy in copies:
        copy.wait()


def swap_matrix():
    i = lax.broadcasted_iota(jnp.int32, (SIDE, SIDE), 0)
    j = lax.broadcasted_iota(jnp.int32, (SIDE, SIDE), 1)
    return (j == (i % ROWS) * ROWS + i // ROWS).astype(jnp.float32).astype(jnp.bfloat16)


def to_matrix(swap, tiles, out_ref, first):
    both = jnp.concatenate(tiles, axis=1)
    for q in range(both.shape[0] // SIDE):
        moved = jnp.dot(swap, both[q * SIDE : (q + 1) * SIDE], preferred_element_type=jnp.float32)
        moved = moved.astype(jnp.bfloat16)
        at = pl.ds(first + q * ROWS, ROWS)
        for s in range(ROWS):
            out_ref[at, s * WIDE : (s + 1) * WIDE] = moved[s * ROWS : (s + 1) * ROWS]


def lam_kernel(where_ref, *refs):
    part_refs, (out_ref, panel_ref) = refs[:STEPS], refs[STEPS:]
    z4, y = where_ref[1], where_ref[2]
    for n, part_ref in enumerate(part_refs):
        for k in range(STEPS):
            panel_ref[((z4 ^ n) * STEPS + (y ^ k))] = part_ref[k]
    all_panels(panel_ref, out_ref)


def all_panels(parts_ref, out_ref, before=lambda step: None):
    swap = swap_matrix()
    panels, _, panel_size = parts_ref.shape[:3]
    chunk = STEPS * panel_size
    for step in range(panels // STEPS):
        before(step)
        tiles = [parts_ref[STEPS * step : STEPS * (step + 1), tile].reshape(chunk * ROWS, LANES) for tile in range(TILES)]
        to_matrix(swap, tiles, out_ref, step * chunk)


def left_half(shape):
    return lax.broadcasted_iota(jnp.int32, shape, 1) < LANES // 2


def fold(x):
    n = x.shape[0] // 2
    return jnp.where(left_half((n, LANES)), x[:n], pltpu.roll(x[n:], LANES // 2, 1))


def unfold(x):
    return jnp.concatenate([x, pltpu.roll(x, LANES // 2, 1)], axis=0)


def amp_kernel(parts_in, amp_ref, parts_ref, sems):
    copies = []
    for step in range(parts_ref.shape[0] // STEPS):
        some = pl.ds(step * STEPS, STEPS)
        copies.append(pltpu.make_async_copy(parts_in.at[some], parts_ref.at[some], sems.at[step]))
        copies[-1].start()
    all_panels(parts_ref, amp_ref, lambda step: copies[step].wait())


def cross_kernel(where_ref, lam_ref, amp_ref, sym_ref, cross_ref):
    zb = where_ref[0]
    half = lam_ref.shape[0]
    cross_ref[...] = jnp.zeros_like(cross_ref)
    for n, which in enumerate((zb, 1 - zb)):
        amp = amp_ref[pl.ds(pl.multiple_of(which * half, half), half)]
        cross_ref[n, :half, :half] = lax.dot_general(
            lam_ref[...], amp, (((1,), (1,)), ((), ())), preferred_element_type=jnp.float32
        )
    within, between = cross_ref[0], cross_ref[1]
    within = 0.5 * (within + within.T)
    between = 0.5 * jnp.where(zb == 0, between, between.T)
    at = 0
    for rows in (
        between[:half, :LANES],
        fold(between[:half, LANES:]),
        within[:LANES, :LANES],
        fold(within[:LANES, LANES:]),
        fold(within[LANES:half, LANES:]),
    ):
        sym_ref[at : at + rows.shape[0]] = rows
        at += rows.shape[0]


def density_kernel(where_ref, sym_ref, listed_ref, amp_ref, out_ref, square_ref, inter_ref, flat_ref):
    pairs, depth = amp_ref.shape
    half = flat_ref.shape[0]
    panels = listed_ref.shape[0]
    panel_size = pairs // panels
    zb = where_ref[0]

    def spread(first_row, rows):
        row = first_row + lax.broadcasted_iota(jnp.int32, (rows, panels), 0)
        first = lax.broadcasted_iota(jnp.int32, (rows, panels), 1) * panel_size
        return ((row >= first) & (row < first + panel_size)).astype(jnp.float32)

    mask = jnp.dot(spread(zb * half, half), listed_ref[...], preferred_element_type=jnp.float32)
    mask = lax.dot_general(mask, spread(0, pairs), (((1,), (1,)), ((), ())), preferred_element_type=jnp.float32)

    sizes = [half, half // 2, LANES, LANES // 2, (half - LANES) // 2]
    ends = [sum(sizes[: n + 1]) for n in range(len(sizes))]
    x, x_right, w, w_right, w_last = (sym_ref[e - n : e].astype(jnp.float32) for e, n in zip(ends, sizes))
    square_ref[...] = jnp.zeros_like(square_ref)
    square_ref[:half, :LANES] = x
    square_ref[:half, LANES:] = unfold(x_right)
    between = jnp.where(zb == 0, square_ref[...], square_ref[...].T)[:half]
    w_right = unfold(w_right)
    square_ref[:LANES, :LANES] = w
    square_ref[:LANES, LANES:] = w_right
    square_ref[LANES:half, :LANES] = w_right.T[: half - LANES]
    square_ref[LANES:half, LANES:] = unfold(w_last)
    within = square_ref[:half]
    left = jnp.where(zb == 0, within, between)
    right = jnp.where(zb == 0, between, within)
    keep = left_half((half, LANES))
    turned = [pltpu.roll(right[:, n * LANES : (n + 1) * LANES], LANES // 2, 1) for n in range(2)]
    for n, block in enumerate(
        (left[:, :LANES], jnp.where(keep, left[:, LANES:], turned[0]), jnp.where(keep, turned[0], turned[1]))
    ):
        cols = slice(n * LANES, (n + 1) * LANES)
        inter_ref[:, cols] = (block * mask[:, cols]).astype(jnp.bfloat16)
    own = inter_ref[...]
    for c in range(depth // WIDE):
        flat_ref[:, c * WIDE : (c + 1) * WIDE] = jnp.dot(
            own, amp_ref[:, c * WIDE : (c + 1) * WIDE], preferred_element_type=jnp.float32
        ).astype(jnp.bfloat16)
    swap = swap_matrix()

    def relayout(step, carry):
        rows = pl.ds(pl.multiple_of(step * ROWS, ROWS), ROWS)
        both = jnp.concatenate([flat_ref[rows, s * WIDE : (s + 1) * WIDE] for s in range(ROWS)], axis=0)
        moved = jnp.dot(swap, both, preferred_element_type=jnp.float32).astype(jnp.bfloat16)
        for tile in range(TILES):
            out_ref[rows, tile] = moved[:, tile * LANES : (tile + 1) * LANES].reshape(ROWS, ROWS, LANES)
        return carry

    lax.fori_loop(0, half // ROWS, relayout, 0, unroll=True)


def exchange(x, axis):
    return lax.all_to_all(x, axis, split_axis=0, concat_axis=0, tiled=True)


def shifts(parts, axis):
    return [parts[0]] + [
        lax.ppermute(part, axis, [(k, k ^ s) for k in range(STEPS)]) for s, part in enumerate(parts) if s > 0
    ]


def on_device(lambda_amps, t_amps, panel_home, pair_list):
    npanels = lax.axis_size(PAIR)
    panel_size, rows, cols = lambda_amps.shape
    pairs, half = npanels * panel_size, npanels * panel_size // 2
    depth = ROWS * WIDE
    bf16, f32 = jnp.bfloat16, jnp.float32
    folded = half + half // 2 + LANES + LANES // 2 + (half - LANES) // 2
    plane, height = lax.axis_size(PLANE), lax.axis_size(LINE)
    own = folded // plane
    between = lax.axis_index(PLANE) * own < half * half // LANES
    where = [lax.axis_index("zb"), lax.axis_index("z4"), lax.axis_index("y"), between]
    where = jnp.stack([w.astype(jnp.int32) for w in where])

    home = onehot(panel_home, npanels)
    first = jnp.dot(onehot(pair_list[:, 0], npanels), home, precision=lax.Precision.HIGHEST)
    second = jnp.dot(onehot(pair_list[:, 1], npanels), home, precision=lax.Precision.HIGHEST)
    listed = jnp.dot(first.T, second, precision=lax.Precision.HIGHEST)
    listed = jnp.minimum(listed + listed.T, 1.0)

    part = (TILES, panel_size, ROWS, LANES)
    amp_parts = call(pack_amp, jax.ShapeDtypeStruct((npanels,) + part, bf16), (t_amps,), [pltpu.VMEM(t_amps.shape, bf16), dma(2 * npanels + rows // ROWS)], free_in=(0,), free_out=(0,), limit=VMEM_MOST)
    four = [jax.ShapeDtypeStruct((STEPS,) + part, bf16)] * STEPS
    lam_parts = call(pack_lam, four, (where, lambda_amps), scalars=1)
    amp_parts = exchange(amp_parts, PAIR)
    lam_parts = call(regroup, four, (where, *shifts(lam_parts, "y")), scalars=1)
    lam = call(
        lam_kernel,
        jax.ShapeDtypeStruct((half, depth), bf16),
        (where, *shifts(lam_parts, "z4")),
        [pltpu.VMEM((npanels // 2,) + part, bf16)],
        scalars=1,
    )
    matrix = jax.ShapeDtypeStruct((pairs, depth), bf16)
    sym = call(
        cross_kernel,
        jax.ShapeDtypeStruct((folded, LANES), f32),
        (where, lam, call(all_panels, matrix, (amp_parts,))),
        [pltpu.VMEM((2, SQUARE, SQUARE), f32)],
        scalars=1,
    )
    terms = exchange(sym.reshape(plane, own, LANES), PLANE)
    terms = exchange(jnp.broadcast_to(jnp.sum(terms, axis=0), (height, own, LANES)), LINE)
    halves = terms.reshape(2, height // 2, own, LANES).sum(axis=1)
    mine = jnp.where(where[0] == 0, halves[0], halves[1])
    total = jnp.where(where[3] == 1, halves[0] + halves[1], mine).astype(bf16)
    terms = jnp.broadcast_to(total, (plane, own, LANES))
    later, _ = lax.optimization_barrier((amp_parts, total))
    upper = exchange(terms, PLANE)
    brought = [pltpu.VMEM((npanels,) + part, bf16), dma(npanels // STEPS)]
    amp = call(amp_kernel, matrix, (later,), brought, free_in=(0,))
    result = call(
        density_kernel,
        jax.ShapeDtypeStruct((half, TILES, ROWS, LANES), bf16),
        (where, upper.reshape(folded, LANES), listed, amp),
        [pltpu.VMEM((SQUARE, SQUARE), f32), pltpu.VMEM((half, pairs), bf16), pltpu.VMEM((half, depth), bf16)],
        scalars=1,
    )
    result = exchange(result.reshape(npanels // 2, panel_size, TILES, ROWS, LANES), HALF)
    return call(
        unpack, jax.ShapeDtypeStruct(lambda_amps.shape, bf16), (result,), [dma(npanels)], free_in=(0,), free_out=(0,)
    )


def solution(mesh):
    fine = Mesh(mesh.devices.reshape(2, 4, 4, 2, 4, 2), PAIR + VIRT)
    placed = (P(PAIR, VIRT, None), P(PAIR, VIRT, None), P(), P())
    return jax.shard_map(
        on_device, mesh=fine, in_specs=placed, out_specs=P(PAIR, VIRT, None), check_vma=False
    )
```

```python
import jax
import jax.numpy as jnp
from jax import lax
from jax.experimental import pallas as pl
from jax.experimental.pallas import tpu as pltpu
from jax.sharding import Mesh, PartitionSpec as P

HALF = ("z4", "y")
PAIR = ("zb",) + HALF
VIRT = ("zh", "x", "c")
PLANE = ("y", "x", "c")
LINE = ("zb", "z4", "zh")

ROWS = 16
LANES = 128
TILES = 2
WIDE = TILES * LANES
SIDE = ROWS * ROWS
STEPS = 4
SQUARE = 256
VMEM_LIMIT = 48 * 1024 * 1024
VMEM_MOST = 62 * 1024 * 1024


def onehot(index, count):
    return (index[:, None] == jnp.arange(count)[None, :]).astype(jnp.float32)


def call(body, out_shape, args, scratch=(), scalars=0, free_in=(), free_out=(), limit=VMEM_LIMIT):
    many = isinstance(out_shape, (list, tuple))
    outs = out_shape if many else [out_shape]
    smem, vmem, free = (pl.BlockSpec(memory_space=m) for m in (pltpu.SMEM, pltpu.VMEM, pl.ANY))
    out_specs = [free if n in free_out else vmem for n in range(len(outs))]
    return pl.pallas_call(
        body,
        out_shape=out_shape,
        in_specs=[smem] * scalars + [free if n in free_in else vmem for n in range(scalars, len(args))],
        out_specs=out_specs if many else out_specs[0],
        scratch_shapes=list(scratch),
        compiler_params=pltpu.CompilerParams(vmem_limit_bytes=limit),
    )(*args)


def dma(count):
    return pltpu.SemaphoreType.DMA((count,))


def pack_amp(amp_in, out_ref, amp_ref, sems):
    across = amp_ref.shape[2] // WIDE
    down = amp_ref.shape[1] // ROWS
    come, go = [], []
    for i in range(down):
        rows = (slice(None), pl.ds(i * ROWS, ROWS))
        come.append(pltpu.make_async_copy(amp_in.at[rows], amp_ref.at[rows], sems.at[i]))
        come[-1].start()
    for i in range(down):
        come[i].wait()
        for c in range(across):
            for tile in range(TILES):
                part = amp_ref.at[:, pl.ds(i * ROWS, ROWS), pl.ds(c * WIDE + tile * LANES, LANES)]
                for twin in range(2):
                    place = out_ref.at[(twin * down + i) * across + c, tile]
                    go.append(pltpu.make_async_copy(part, place, sems.at[down + len(go)]))
                    go[-1].start()
    for copy in go:
        copy.wait()


def pack_lam(where_ref, lam_ref, *out_refs):
    y = where_ref[2]
    for s, out_ref in enumerate(out_refs):
        for i in range(lam_ref.shape[1] // ROWS):
            for tile in range(TILES):
                at = pl.multiple_of((y ^ s) * WIDE + tile * LANES, LANES)
                out_ref[i, tile] = lam_ref[:, i * ROWS : (i + 1) * ROWS, pl.ds(at, LANES)]


def regroup(where_ref, *refs):
    z4 = where_ref[1]
    ins, outs = refs[:STEPS], refs[STEPS:]
    for u, out_ref in enumerate(outs):
        for s, in_ref in enumerate(ins):
            out_ref[s] = in_ref[z4 ^ u]


def unpack(parts_ref, out_ref, sems):
    across = out_ref.shape[2] // WIDE
    copies = []
    for d in range(parts_ref.shape[0]):
        i, c = divmod(d, across)
        for tile in range(TILES):
            at = c * WIDE + tile * LANES
            part = out_ref.at[:, pl.ds(i * ROWS, ROWS), pl.ds(at, LANES)]
            copies.append(pltpu.make_async_copy(parts_ref.at[d, :, tile], part, sems.at[len(copies)]))
            copies[-1].start()
    for copy in copies:
        copy.wait()


def swap_matrix():
    i = lax.broadcasted_iota(jnp.int32, (SIDE, SIDE), 0)
    j = lax.broadcasted_iota(jnp.int32, (SIDE, SIDE), 1)
    return (j == (i % ROWS) * ROWS + i // ROWS).astype(jnp.float32).astype(jnp.bfloat16)


def to_matrix(swap, tiles, out_ref, first):
    both = jnp.concatenate(tiles, axis=1)
    for q in range(both.shape[0] // SIDE):
        moved = jnp.dot(swap, both[q * SIDE : (q + 1) * SIDE], preferred_element_type=jnp.float32)
        moved = moved.astype(jnp.bfloat16)
        at = pl.ds(first + q * ROWS, ROWS)
        for s in range(ROWS):
            out_ref[at, s * WIDE : (s + 1) * WIDE] = moved[s * ROWS : (s + 1) * ROWS]


def lam_kernel(where_ref, *refs):
    part_refs, (out_ref, panel_ref) = refs[:STEPS], refs[STEPS:]
    z4, y = where_ref[1], where_ref[2]
    for n, part_ref in enumerate(part_refs):
        for k in range(STEPS):
            panel_ref[((z4 ^ n) * STEPS + (y ^ k))] = part_ref[k]
    all_panels(panel_ref, out_ref)


def all_panels(parts_ref, out_ref, before=lambda step: None):
    swap = swap_matrix()
    panels, _, panel_size = parts_ref.shape[:3]
    chunk = STEPS * panel_size
    for step in range(panels // STEPS):
        before(step)
        tiles = [parts_ref[STEPS * step : STEPS * (step + 1), tile].reshape(chunk * ROWS, LANES) for tile in range(TILES)]
        to_matrix(swap, tiles, out_ref, step * chunk)


def left_half(shape):
    return lax.broadcasted_iota(jnp.int32, shape, 1) < LANES // 2


def fold(x):
    n = x.shape[0] // 2
    return jnp.where(left_half((n, LANES)), x[:n], pltpu.roll(x[n:], LANES // 2, 1))


def unfold(x):
    return jnp.concatenate([x, pltpu.roll(x, LANES // 2, 1)], axis=0)


def amp_kernel(where_ref, parts_in, listed_ref, amp_ref, mask_ref, parts_ref, sems):
    copies = []
    for step in range(parts_ref.shape[0] // STEPS):
        some = pl.ds(step * STEPS, STEPS)
        copies.append(pltpu.make_async_copy(parts_in.at[some], parts_ref.at[some], sems.at[step]))
        copies[-1].start()
    half, pairs = mask_ref.shape
    panels = listed_ref.shape[0]
    panel_size = pairs // panels
    zb = where_ref[0]

    def spread(first_row, rows):
        row = first_row + lax.broadcasted_iota(jnp.int32, (rows, panels), 0)
        first = lax.broadcasted_iota(jnp.int32, (rows, panels), 1) * panel_size
        return ((row >= first) & (row < first + panel_size)).astype(jnp.float32)

    mask = jnp.dot(spread(zb * half, half), listed_ref[...], preferred_element_type=jnp.float32)
    mask_ref[...] = lax.dot_general(mask, spread(0, pairs), (((1,), (1,)), ((), ())), preferred_element_type=jnp.float32)
    all_panels(parts_ref, amp_ref, lambda step: copies[step].wait())


def cross_kernel(where_ref, lam_ref, amp_ref, sym_ref, cross_ref):
    zb = where_ref[0]
    half = lam_ref.shape[0]
    cross_ref[...] = jnp.zeros_like(cross_ref)
    for n, which in enumerate((zb, 1 - zb)):
        amp = amp_ref[pl.ds(pl.multiple_of(which * half, half), half)]
        cross_ref[n, :half, :half] = lax.dot_general(
            lam_ref[...], amp, (((1,), (1,)), ((), ())), preferred_element_type=jnp.float32
        )
    within, between = cross_ref[0], cross_ref[1]
    within = 0.5 * (within + within.T)
    between = 0.5 * jnp.where(zb == 0, between, between.T)
    at = 0
    for rows in (
        between[:half, :LANES],
        fold(between[:half, LANES:]),
        within[:LANES, :LANES],
        fold(within[:LANES, LANES:]),
        fold(within[LANES:half, LANES:]),
    ):
        sym_ref[at : at + rows.shape[0]] = rows
        at += rows.shape[0]


def density_kernel(where_ref, sym_ref, mask_ref, amp_ref, out_ref, square_ref, inter_ref, flat_ref):
    pairs, depth = amp_ref.shape
    half = flat_ref.shape[0]
    zb = where_ref[0]
    sizes = [half, half // 2, LANES, LANES // 2, (half - LANES) // 2]
    ends = [sum(sizes[: n + 1]) for n in range(len(sizes))]
    x, x_right, w, w_right, w_last = (sym_ref[e - n : e].astype(jnp.float32) for e, n in zip(ends, sizes))
    square_ref[...] = jnp.zeros_like(square_ref)
    square_ref[:half, :LANES] = x
    square_ref[:half, LANES:] = unfold(x_right)
    between = jnp.where(zb == 0, square_ref[...], square_ref[...].T)[:half]
    w_right = unfold(w_right)
    square_ref[:LANES, :LANES] = w
    square_ref[:LANES, LANES:] = w_right
    square_ref[LANES:half, :LANES] = w_right.T[: half - LANES]
    square_ref[LANES:half, LANES:] = unfold(w_last)
    within = square_ref[:half]
    left = jnp.where(zb == 0, within, between)
    right = jnp.where(zb == 0, between, within)
    keep = left_half((half, LANES))
    turned = [pltpu.roll(right[:, n * LANES : (n + 1) * LANES], LANES // 2, 1) for n in range(2)]
    for n, block in enumerate(
        (left[:, :LANES], jnp.where(keep, left[:, LANES:], turned[0]), jnp.where(keep, turned[0], turned[1]))
    ):
        cols = slice(n * LANES, (n + 1) * LANES)
        inter_ref[:, cols] = (block * mask_ref[:, cols]).astype(jnp.bfloat16)
    own = inter_ref[...]
    for c in range(depth // WIDE):
        flat_ref[:, c * WIDE : (c + 1) * WIDE] = jnp.dot(
            own, amp_ref[:, c * WIDE : (c + 1) * WIDE], preferred_element_type=jnp.float32
        ).astype(jnp.bfloat16)
    swap = swap_matrix()

    def relayout(step, carry):
        rows = pl.ds(pl.multiple_of(step * ROWS, ROWS), ROWS)
        both = jnp.concatenate([flat_ref[rows, s * WIDE : (s + 1) * WIDE] for s in range(ROWS)], axis=0)
        moved = jnp.dot(swap, both, preferred_element_type=jnp.float32).astype(jnp.bfloat16)
        for tile in range(TILES):
            out_ref[rows, tile] = moved[:, tile * LANES : (tile + 1) * LANES].reshape(ROWS, ROWS, LANES)
        return carry

    lax.fori_loop(0, half // ROWS, relayout, 0, unroll=True)


def exchange(x, axis):
    return lax.all_to_all(x, axis, split_axis=0, concat_axis=0, tiled=True)


def shifts(parts, axis):
    return [parts[0]] + [
        lax.ppermute(part, axis, [(k, k ^ s) for k in range(STEPS)]) for s, part in enumerate(parts) if s > 0
    ]


def on_device(lambda_amps, t_amps, panel_home, pair_list):
    npanels = lax.axis_size(PAIR)
    panel_size, rows, cols = lambda_amps.shape
    pairs, half = npanels * panel_size, npanels * panel_size // 2
    depth = ROWS * WIDE
    bf16, f32 = jnp.bfloat16, jnp.float32
    folded = half + half // 2 + LANES + LANES // 2 + (half - LANES) // 2
    plane, height = lax.axis_size(PLANE), lax.axis_size(LINE)
    own = folded // plane
    between = lax.axis_index(PLANE) * own < half * half // LANES
    where = [lax.axis_index("zb"), lax.axis_index("z4"), lax.axis_index("y"), between]
    where = jnp.stack([w.astype(jnp.int32) for w in where])

    home = onehot(panel_home, npanels)
    first = jnp.dot(onehot(pair_list[:, 0], npanels), home, precision=lax.Precision.HIGHEST)
    second = jnp.dot(onehot(pair_list[:, 1], npanels), home, precision=lax.Precision.HIGHEST)
    listed = jnp.dot(first.T, second, precision=lax.Precision.HIGHEST)
    listed = jnp.minimum(listed + listed.T, 1.0)

    part = (TILES, panel_size, ROWS, LANES)
    amp_parts = call(pack_amp, jax.ShapeDtypeStruct((npanels,) + part, bf16), (t_amps,), [pltpu.VMEM(t_amps.shape, bf16), dma(2 * npanels + rows // ROWS)], free_in=(0,), free_out=(0,), limit=VMEM_MOST)
    four = [jax.ShapeDtypeStruct((STEPS,) + part, bf16)] * STEPS
    lam_parts = call(pack_lam, four, (where, lambda_amps), scalars=1)
    amp_parts = exchange(amp_parts, PAIR)
    lam_parts = call(regroup, four, (where, *shifts(lam_parts, "y")), scalars=1)
    lam = call(
        lam_kernel,
        jax.ShapeDtypeStruct((half, depth), bf16),
        (where, *shifts(lam_parts, "z4")),
        [pltpu.VMEM((npanels // 2,) + part, bf16)],
        scalars=1,
    )
    matrix = jax.ShapeDtypeStruct((pairs, depth), bf16)
    sym = call(
        cross_kernel,
        jax.ShapeDtypeStruct((folded, LANES), f32),
        (where, lam, call(all_panels, matrix, (amp_parts,))),
        [pltpu.VMEM((2, SQUARE, SQUARE), f32)],
        scalars=1,
    )
    terms = exchange(sym.reshape(plane, own, LANES), PLANE)
    terms = exchange(jnp.broadcast_to(jnp.sum(terms, axis=0), (height, own, LANES)), LINE)
    halves = terms.reshape(2, height // 2, own, LANES).sum(axis=1)
    mine = jnp.where(where[0] == 0, halves[0], halves[1])
    total = jnp.where(where[3] == 1, halves[0] + halves[1], mine).astype(bf16)
    terms = jnp.broadcast_to(total, (plane, own, LANES))
    later, _ = lax.optimization_barrier((amp_parts, total))
    upper = exchange(terms, PLANE)
    brought = [pltpu.VMEM((npanels,) + part, bf16), dma(npanels // STEPS)]
    mask = jax.ShapeDtypeStruct((half, pairs), f32)
    amp, mask = call(amp_kernel, [matrix, mask], (where, later, listed), brought, scalars=1, free_in=(1,))
    result = call(
        density_kernel,
        jax.ShapeDtypeStruct((half, TILES, ROWS, LANES), bf16),
        (where, upper.reshape(folded, LANES), mask, amp),
        [pltpu.VMEM((SQUARE, SQUARE), f32), pltpu.VMEM((half, pairs), bf16), pltpu.VMEM((half, depth), bf16)],
        scalars=1,
    )
    result = exchange(result.reshape(npanels // 2, panel_size, TILES, ROWS, LANES), HALF)
    return call(
        unpack, jax.ShapeDtypeStruct(lambda_amps.shape, bf16), (result,), [dma(npanels)], free_in=(0,), free_out=(0,)
    )


def solution(mesh):
    fine = Mesh(mesh.devices.reshape(2, 4, 4, 2, 4, 2), PAIR + VIRT)
    placed = (P(PAIR, VIRT, None), P(PAIR, VIRT, None), P(), P())
    return jax.shard_map(
        on_device, mesh=fine, in_specs=placed, out_specs=P(PAIR, VIRT, None), check_vma=False
    )
```

```python
import jax
import jax.numpy as jnp
from jax import lax
from jax.experimental import pallas as pl
from jax.experimental.pallas import tpu as pltpu
from jax.sharding import Mesh, PartitionSpec as P

HALF = ("z4", "y")
PAIR = ("zb",) + HALF
VIRT = ("zh", "x", "c")
PLANE = ("c", "y", "x")
LINE = ("zh", "zb", "z4")

ROWS = 16
LANES = 128
TILES = 2
WIDE = TILES * LANES
SIDE = ROWS * ROWS
STEPS = 4
SQUARE = 256
VMEM_LIMIT = 48 * 1024 * 1024
VMEM_MOST = 62 * 1024 * 1024


def onehot(index, count):
    return (index[:, None] == jnp.arange(count)[None, :]).astype(jnp.float32)


def call(body, out_shape, args, scratch=(), scalars=0, free_in=(), free_out=(), limit=VMEM_LIMIT):
    many = isinstance(out_shape, (list, tuple))
    outs = out_shape if many else [out_shape]
    smem, vmem, free = (pl.BlockSpec(memory_space=m) for m in (pltpu.SMEM, pltpu.VMEM, pl.ANY))
    out_specs = [free if n in free_out else vmem for n in range(len(outs))]
    return pl.pallas_call(
        body,
        out_shape=out_shape,
        in_specs=[smem] * scalars + [free if n in free_in else vmem for n in range(scalars, len(args))],
        out_specs=out_specs if many else out_specs[0],
        scratch_shapes=list(scratch),
        compiler_params=pltpu.CompilerParams(vmem_limit_bytes=limit),
    )(*args)


def dma(count):
    return pltpu.SemaphoreType.DMA((count,))


def pack_amp(amp_in, out_ref, amp_ref, sems):
    across = amp_ref.shape[2] // WIDE
    down = amp_ref.shape[1] // ROWS
    come, go = [], []
    for i in range(down):
        rows = (slice(None), pl.ds(i * ROWS, ROWS))
        come.append(pltpu.make_async_copy(amp_in.at[rows], amp_ref.at[rows], sems.at[i]))
        come[-1].start()
    for i in range(down):
        come[i].wait()
        for c in range(across):
            for tile in range(TILES):
                part = amp_ref.at[:, pl.ds(i * ROWS, ROWS), pl.ds(c * WIDE + tile * LANES, LANES)]
                for twin in range(2):
                    place = out_ref.at[(twin * down + i) * across + c, tile]
                    go.append(pltpu.make_async_copy(part, place, sems.at[down + len(go)]))
                    go[-1].start()
    for copy in go:
        copy.wait()


def pack_lam(where_ref, lam_ref, *out_refs):
    y = where_ref[2]
    for s, out_ref in enumerate(out_refs):
        for i in range(lam_ref.shape[1] // ROWS):
            for tile in range(TILES):
                at = pl.multiple_of((y ^ s) * WIDE + tile * LANES, LANES)
                out_ref[i, tile] = lam_ref[:, i * ROWS : (i + 1) * ROWS, pl.ds(at, LANES)]


def regroup(where_ref, *refs):
    z4 = where_ref[1]
    ins, outs = refs[:STEPS], refs[STEPS:]
    for u, out_ref in enumerate(outs):
        for s, in_ref in enumerate(ins):
            out_ref[s] = in_ref[z4 ^ u]


def unpack(parts_ref, out_ref, sems):
    across = out_ref.shape[2] // WIDE
    copies = []
    for d in range(parts_ref.shape[0]):
        i, c = divmod(d, across)
        for tile in range(TILES):
            at = c * WIDE + tile * LANES
            part = out_ref.at[:, pl.ds(i * ROWS, ROWS), pl.ds(at, LANES)]
            copies.append(pltpu.make_async_copy(parts_ref.at[d, :, tile], part, sems.at[len(copies)]))
            copies[-1].start()
    for copy in copies:
        copy.wait()


def swap_matrix():
    i = lax.broadcasted_iota(jnp.int32, (SIDE, SIDE), 0)
    j = lax.broadcasted_iota(jnp.int32, (SIDE, SIDE), 1)
    return (j == (i % ROWS) * ROWS + i // ROWS).astype(jnp.float32).astype(jnp.bfloat16)


def to_matrix(swap, tiles, out_ref, first):
    both = jnp.concatenate(tiles, axis=1)
    for q in range(both.shape[0] // SIDE):
        moved = jnp.dot(swap, both[q * SIDE : (q + 1) * SIDE], preferred_element_type=jnp.float32)
        moved = moved.astype(jnp.bfloat16)
        at = pl.ds(first + q * ROWS, ROWS)
        for s in range(ROWS):
            out_ref[at, s * WIDE : (s + 1) * WIDE] = moved[s * ROWS : (s + 1) * ROWS]


def lam_kernel(where_ref, *refs):
    part_refs, (out_ref, panel_ref) = refs[:STEPS], refs[STEPS:]
    z4, y = where_ref[1], where_ref[2]
    for n, part_ref in enumerate(part_refs):
        for k in range(STEPS):
            panel_ref[((z4 ^ n) * STEPS + (y ^ k))] = part_ref[k]
    all_panels(panel_ref, out_ref)


def all_panels(parts_ref, out_ref, before=lambda step: None):
    swap = swap_matrix()
    panels, _, panel_size = parts_ref.shape[:3]
    chunk = STEPS * panel_size
    for step in range(panels // STEPS):
        before(step)
        tiles = [parts_ref[STEPS * step : STEPS * (step + 1), tile].reshape(chunk * ROWS, LANES) for tile in range(TILES)]
        to_matrix(swap, tiles, out_ref, step * chunk)


def left_half(shape):
    return lax.broadcasted_iota(jnp.int32, shape, 1) < LANES // 2


def fold(x):
    n = x.shape[0] // 2
    return jnp.where(left_half((n, LANES)), x[:n], pltpu.roll(x[n:], LANES // 2, 1))


def unfold(x):
    return jnp.concatenate([x, pltpu.roll(x, LANES // 2, 1)], axis=0)


def amp_kernel(parts_in, amp_ref, parts_ref, sems):
    copies = []
    for step in range(parts_ref.shape[0] // STEPS):
        some = pl.ds(step * STEPS, STEPS)
        copies.append(pltpu.make_async_copy(parts_in.at[some], parts_ref.at[some], sems.at[step]))
        copies[-1].start()
    all_panels(parts_ref, amp_ref, lambda step: copies[step].wait())


def cross_kernel(where_ref, lam_ref, amp_ref, sym_ref, cross_ref):
    zb = where_ref[0]
    half = lam_ref.shape[0]
    cross_ref[...] = jnp.zeros_like(cross_ref)
    for n, which in enumerate((zb, 1 - zb)):
        amp = amp_ref[pl.ds(pl.multiple_of(which * half, half), half)]
        cross_ref[n, :half, :half] = lax.dot_general(
            lam_ref[...], amp, (((1,), (1,)), ((), ())), preferred_element_type=jnp.float32
        )
    within, between = cross_ref[0], cross_ref[1]
    within = 0.5 * (within + within.T)
    between = 0.5 * jnp.where(zb == 0, between, between.T)
    at = 0
    for rows in (
        between[:half, :LANES],
        fold(between[:half, LANES:]),
        within[:LANES, :LANES],
        fold(within[:LANES, LANES:]),
        fold(within[LANES:half, LANES:]),
    ):
        sym_ref[at : at + rows.shape[0]] = rows
        at += rows.shape[0]


def density_kernel(where_ref, sym_ref, listed_ref, amp_ref, out_ref, square_ref, inter_ref, flat_ref):
    pairs, depth = amp_ref.shape
    half = flat_ref.shape[0]
    panels = listed_ref.shape[0]
    panel_size = pairs // panels
    zb = where_ref[0]

    def spread(first_row, rows):
        row = first_row + lax.broadcasted_iota(jnp.int32, (rows, panels), 0)
        first = lax.broadcasted_iota(jnp.int32, (rows, panels), 1) * panel_size
        return ((row >= first) & (row < first + panel_size)).astype(jnp.float32)

    mask = jnp.dot(spread(zb * half, half), listed_ref[...], preferred_element_type=jnp.float32)
    mask = lax.dot_general(mask, spread(0, pairs), (((1,), (1,)), ((), ())), preferred_element_type=jnp.float32)

    sizes = [half, half // 2, LANES, LANES // 2, (half - LANES) // 2]
    ends = [sum(sizes[: n + 1]) for n in range(len(sizes))]
    x, x_right, w, w_right, w_last = (sym_ref[e - n : e].astype(jnp.float32) for e, n in zip(ends, sizes))
    square_ref[...] = jnp.zeros_like(square_ref)
    square_ref[:half, :LANES] = x
    square_ref[:half, LANES:] = unfold(x_right)
    between = jnp.where(zb == 0, square_ref[...], square_ref[...].T)[:half]
    w_right = unfold(w_right)
    square_ref[:LANES, :LANES] = w
    square_ref[:LANES, LANES:] = w_right
    square_ref[LANES:half, :LANES] = w_right.T[: half - LANES]
    square_ref[LANES:half, LANES:] = unfold(w_last)
    within = square_ref[:half]
    left = jnp.where(zb == 0, within, between)
    right = jnp.where(zb == 0, between, within)
    keep = left_half((half, LANES))
    turned = [pltpu.roll(right[:, n * LANES : (n + 1) * LANES], LANES // 2, 1) for n in range(2)]
    for n, block in enumerate(
        (left[:, :LANES], jnp.where(keep, left[:, LANES:], turned[0]), jnp.where(keep, turned[0], turned[1]))
    ):
        cols = slice(n * LANES, (n + 1) * LANES)
        inter_ref[:, cols] = (block * mask[:, cols]).astype(jnp.bfloat16)
    own = inter_ref[...]
    for c in range(depth // WIDE):
        flat_ref[:, c * WIDE : (c + 1) * WIDE] = jnp.dot(
            own, amp_ref[:, c * WIDE : (c + 1) * WIDE], preferred_element_type=jnp.float32
        ).astype(jnp.bfloat16)
    swap = swap_matrix()

    def relayout(step, carry):
        rows = pl.ds(pl.multiple_of(step * ROWS, ROWS), ROWS)
        both = jnp.concatenate([flat_ref[rows, s * WIDE : (s + 1) * WIDE] for s in range(ROWS)], axis=0)
        moved = jnp.dot(swap, both, preferred_element_type=jnp.float32).astype(jnp.bfloat16)
        for tile in range(TILES):
            out_ref[rows, tile] = moved[:, tile * LANES : (tile + 1) * LANES].reshape(ROWS, ROWS, LANES)
        return carry

    lax.fori_loop(0, half // ROWS, relayout, 0, unroll=True)


def exchange(x, axis):
    return lax.all_to_all(x, axis, split_axis=0, concat_axis=0, tiled=True)


def shifts(parts, axis):
    return [parts[0]] + [
        lax.ppermute(part, axis, [(k, k ^ s) for k in range(STEPS)]) for s, part in enumerate(parts) if s > 0
    ]


def on_device(lambda_amps, t_amps, panel_home, pair_list):
    npanels = lax.axis_size(PAIR)
    panel_size, rows, cols = lambda_amps.shape
    pairs, half = npanels * panel_size, npanels * panel_size // 2
    depth = ROWS * WIDE
    bf16, f32 = jnp.bfloat16, jnp.float32
    folded = half + half // 2 + LANES + LANES // 2 + (half - LANES) // 2
    plane, height = lax.axis_size(PLANE), lax.axis_size(LINE)
    own = folded // plane
    between = lax.axis_index(PLANE) * own < half * half // LANES
    where = [lax.axis_index("zb"), lax.axis_index("z4"), lax.axis_index("y"), between]
    where = jnp.stack([w.astype(jnp.int32) for w in where])

    home = onehot(panel_home, npanels)
    first = jnp.dot(onehot(pair_list[:, 0], npanels), home, precision=lax.Precision.HIGHEST)
    second = jnp.dot(onehot(pair_list[:, 1], npanels), home, precision=lax.Precision.HIGHEST)
    listed = jnp.dot(first.T, second, precision=lax.Precision.HIGHEST)
    listed = jnp.minimum(listed + listed.T, 1.0)

    part = (TILES, panel_size, ROWS, LANES)
    amp_parts = call(pack_amp, jax.ShapeDtypeStruct((npanels,) + part, bf16), (t_amps,), [pltpu.VMEM(t_amps.shape, bf16), dma(2 * npanels + rows // ROWS)], free_in=(0,), free_out=(0,), limit=VMEM_MOST)
    four = [jax.ShapeDtypeStruct((STEPS,) + part, bf16)] * STEPS
    lam_parts = call(pack_lam, four, (where, lambda_amps), scalars=1)
    amp_parts = exchange(amp_parts, PAIR)
    lam_parts = call(regroup, four, (where, *shifts(lam_parts, "y")), scalars=1)
    lam = call(
        lam_kernel,
        jax.ShapeDtypeStruct((half, depth), bf16),
        (where, *shifts(lam_parts, "z4")),
        [pltpu.VMEM((npanels // 2,) + part, bf16)],
        scalars=1,
    )
    matrix = jax.ShapeDtypeStruct((pairs, depth), bf16)
    sym = call(
        cross_kernel,
        jax.ShapeDtypeStruct((folded, LANES), f32),
        (where, lam, call(all_panels, matrix, (amp_parts,))),
        [pltpu.VMEM((2, SQUARE, SQUARE), f32)],
        scalars=1,
    )
    terms = exchange(sym.reshape(plane, own, LANES), PLANE)
    terms = exchange(jnp.broadcast_to(jnp.sum(terms, axis=0), (height, own, LANES)), LINE)
    halves = terms.reshape(2, 2, height // 4, own, LANES).sum(axis=(0, 2))
    mine = jnp.where(where[0] == 0, halves[0], halves[1])
    total = jnp.where(where[3] == 1, halves[0] + halves[1], mine).astype(bf16)
    terms = jnp.broadcast_to(total, (plane, own, LANES))
    later, _ = lax.optimization_barrier((amp_parts, total))
    upper = exchange(terms, PLANE)
    brought = [pltpu.VMEM((npanels,) + part, bf16), dma(npanels // STEPS)]
    amp = call(amp_kernel, matrix, (later,), brought, free_in=(0,))
    result = call(
        density_kernel,
        jax.ShapeDtypeStruct((half, TILES, ROWS, LANES), bf16),
        (where, upper.reshape(folded, LANES), listed, amp),
        [pltpu.VMEM((SQUARE, SQUARE), f32), pltpu.VMEM((half, pairs), bf16), pltpu.VMEM((half, depth), bf16)],
        scalars=1,
    )
    result = exchange(result.reshape(npanels // 2, panel_size, TILES, ROWS, LANES), HALF)
    return call(
        unpack, jax.ShapeDtypeStruct(lambda_amps.shape, bf16), (result,), [dma(npanels)], free_in=(0,), free_out=(0,)
    )


def solution(mesh):
    fine = Mesh(mesh.devices.reshape(2, 4, 4, 2, 4, 2), PAIR + VIRT)
    placed = (P(PAIR, VIRT, None), P(PAIR, VIRT, None), P(), P())
    return jax.shard_map(
        on_device, mesh=fine, in_specs=placed, out_specs=P(PAIR, VIRT, None), check_vma=False
    )
```
